32 devices in a mesh: shot: 4 (over x, core), beam: 8 (over z, y).
Axes of the slice: x: 2, y: 2, z: 4, core: 2. Of those that a mesh axis runs over, the one named last changes fastest.
Arguments:
- traces: bfloat16 [4, 2048, 128], P('shot', 'beam'), may hold values from -6 to 6
- send_table: int32 [4, 8, 8, 32], P('shot'), may hold values from 0 to 255
- window_slots: int32 [4, 64, 32], P('shot', 'beam'), may hold values from 0 to 255
- ray_depth: float32 [4, 2048, 32, 128], P('shot', 'beam'), may hold values from 0 to 0.25
- ray_lateral: float32 [2048, 32, 128], P('beam'), may hold values from 0 to 0.25
- ray_spread: float32 [2048, 32, 128], P('beam'), may hold values from 0.0001 to 0.004
- ray_index: int32 [64, 12], P('beam'), may hold values from 0 to 255
- foot_count: int32 [8, 8], P('beam'), may hold values from 1 to 12, 80 in all within a row
- foot_tiles: int32 [64, 12], replicated, may hold values from 0 to 127, as said below
- tile_owner: int32 [128], replicated, may hold values from 0 to 31, as said below
Outputs:
- image_tiles: float32 [128, 128, 128], P(('shot', 'beam'))
The draws below stay inside these ranges and needn't reach their ends.
Inputs may be any that keep to these rules, and one draw needn't show every extreme that they name: `send_table`: entry [s, j, g, i] is a row among the traces of shot gather s held by beam index j. `window_slots`: a slot of the block that the centre's group received, numbered source by source. `ray_index`: a row within the ray table of the centre's group. `foot_count`: the 8 counts of each group sum to 80. `foot_tiles`: entries past a centre's count hold tiles too; one centre's entries have distinct owners; within one group, entries whose tiles have the same owner name the same tile. `tile_owner`: each owner holds exactly 4 tiles.
All inputs are finite; a program needn't handle non-finite values.
Results may differ from the reference program's by a relative error of at most 0.0048.
Values may be sent and summed in bfloat16 or wider, within the bound.
No kernel may reach another device: no remote copies, remote signals or barrier semaphores. Data moves between devices by JAX's collectives and lax.ppermute only.
A program may use at most 192 MiB of HBM per device.

```python
import math
import jax
import jax.numpy as jnp
import numpy as np
from jax import lax

FREQUENCIES = 64
DIRECTIONS = 32
WINDOW = 32
DEPTH_CELLS = 128
LATERAL_CELLS = 128
FOOT_SLOTS = 12
CENTRE_DEV = 8
TRACE_DEV = 256
RAY_ROWS = 256
TILE_DEV = 4
LIVE_DEV = 80
SHOT_GATHERS = 4
GROUPS = 8
OWNERS = 32
CENTRES = 64
TRACES_SHOT = 2048
RAY_TOTAL = 2048
IMAGE_TILES = 128
CAPACITY = 32


def footprint_tables(key):
    permuted = jax.random.permutation(jax.random.fold_in(key, 11), IMAGE_TILES).astype(jnp.int32)
    owner_of = permuted // TILE_DEV
    inverse = jnp.zeros((IMAGE_TILES,), jnp.int32).at[permuted].set(jnp.arange(IMAGE_TILES, dtype=jnp.int32))
    slot_pick = jax.random.randint(jax.random.fold_in(key, 12), (GROUPS, OWNERS), 0, TILE_DEV).astype(jnp.int32)
    last_owner = owner_of[IMAGE_TILES - 1]
    first_owner = owner_of[0]
    slot_pick = slot_pick.at[0, last_owner].set(permuted[IMAGE_TILES - 1] % TILE_DEV)
    slot_pick = slot_pick.at[1, first_owner].set(permuted[0] % TILE_DEV)
    candidate = inverse[jnp.arange(OWNERS, dtype=jnp.int32)[None, :] * TILE_DEV + slot_pick]
    scores = jax.random.randint(jax.random.fold_in(key, 13), (CENTRES, OWNERS), 0, 1 << 20).astype(jnp.int32) * OWNERS + jnp.arange(OWNERS, dtype=jnp.int32)[None, :]
    scores = scores.at[0, last_owner].set(-1)
    scores = scores.at[CENTRE_DEV, first_owner].set(-1)
    chosen = jnp.argsort(scores, axis=1, stable=True)[:, :FOOT_SLOTS]
    centre_group = jnp.arange(CENTRES, dtype=jnp.int32) // CENTRE_DEV
    tile_ids = candidate[centre_group[:, None], chosen]
    return (tile_ids.astype(jnp.int32), owner_of.astype(jnp.int32))


def draw_foot_tiles(key, part):
    return footprint_tables(key)[0]


def draw_tile_owner(key, part):
    return footprint_tables(key)[1]


def place_ends(values, stream_key, low, high):
    extent = values.shape
    spot = [jax.random.randint(jax.random.fold_in(stream_key, axis), (), 0, extent[axis]) for axis in range(len(extent))]
    values = values.at[tuple(spot)].set(low)
    longest = extent.index(max(extent))
    spot[longest] = (spot[longest] + 1) % extent[longest]
    return values.at[tuple(spot)].set(high)


def shard_levels(own_key, extent, cuts, low, high):
    loudness = 1.0
    for dim, shards_of in cuts:
        heights = jax.random.uniform(jax.random.fold_in(jax.random.fold_in(own_key, 6), dim), (shards_of,), jnp.float32, low / len(cuts), high / len(cuts))
        loudness = loudness * jnp.repeat(jnp.exp(heights), extent[dim] // shards_of).reshape((-1,) + (1,) * (len(extent) - 1 - dim))
    return loudness


def profile(count, total, most, slope):
    weights = [(1 << 20) // math.isqrt(rank ** slope) + 1 for rank in range(2, count + 1)]
    surplus, holding = total - most - (count - 1), [1] * (count - 1)
    while surplus > 0:
        movable = [i for i in range(count - 1) if holding[i] < most]
        pool, left = sum([weights[i] for i in movable]), surplus
        for i in movable:
            extra = min(most - holding[i], max(1, left * weights[i] // pool), surplus)
            holding[i] = holding[i] + extra
            surplus = surplus - extra
    return np.array([most] + holding)


def uneven_parts(stream_key, count, total, reach, skew):
    if count == 2:
        one = jax.random.randint(stream_key, (), max(1, total - reach), min(reach, total - 1) + 1)
        return jnp.stack([one, total - one])
    tallies = jnp.asarray(profile(count, total, reach, skew), jnp.int32)
    pairs = (count - 1) // 2
    source_of, sink = tallies[1:1 + 2 * pairs:2], tallies[2:2 + 2 * pairs:2]
    slack = jnp.minimum(source_of - 1, reach - sink)
    shifted = jax.random.randint(jax.random.fold_in(stream_key, 1), (pairs,), 0, 1 << 20) % (slack + 1)
    tallies = tallies.at[1:1 + 2 * pairs:2].set(source_of - shifted).at[2:2 + 2 * pairs:2].set(sink + shifted)
    return tallies[jax.random.permutation(jax.random.fold_in(stream_key, 2), count)]


def normal_values(own_key, dims, deviation, bound, shards=(), kind=jnp.bfloat16):
    loudness = shard_levels(own_key, dims, shards, -0.22, 0.18) if shards else 1.0
    result = jax.random.normal(own_key, dims, jnp.float32) * deviation * loudness
    return jnp.minimum(jnp.maximum(result, -bound), bound).astype(kind)


def setup_inputs(seed: int = 0) -> dict:
    streams_of = jax.random.split(jax.random.key(seed), 11)
    traces = normal_values(streams_of[0], (SHOT_GATHERS, TRACES_SHOT, 2 * FREQUENCIES), 1.0, 6.0, ((0, 4), (1, 8)))
    send_table = place_ends(jax.random.randint(streams_of[1], (SHOT_GATHERS, GROUPS, GROUPS, CAPACITY), 0, TRACE_DEV), jax.random.fold_in(streams_of[1], 1), 0, TRACE_DEV - 1).astype(jnp.int32)
    window_slots = place_ends(jax.random.randint(streams_of[2], (SHOT_GATHERS, CENTRES, WINDOW), 0, GROUPS * CAPACITY), jax.random.fold_in(streams_of[2], 1), 0, (GROUPS * CAPACITY) - 1).astype(jnp.int32)
    ray_depth = jnp.clip(0.25 * jax.random.uniform(streams_of[3], (SHOT_GATHERS, RAY_TOTAL, DIRECTIONS, DEPTH_CELLS), jnp.float32) ** shard_levels(streams_of[3], (SHOT_GATHERS, RAY_TOTAL, DIRECTIONS, DEPTH_CELLS), ((0, 4), (1, 8)), -0.2, 0.2), 0.0, 0.25)
    ray_lateral = jnp.clip(0.25 * jax.random.uniform(streams_of[4], (RAY_TOTAL, DIRECTIONS, LATERAL_CELLS), jnp.float32) ** shard_levels(streams_of[4], (RAY_TOTAL, DIRECTIONS, LATERAL_CELLS), ((0, 8),), -0.2, 0.2), 0.0, 0.25)
    ray_spread = jnp.clip(jnp.exp(math.log(0.004) - 3.6888795 * jax.random.uniform(streams_of[5], (RAY_TOTAL, DIRECTIONS, LATERAL_CELLS), jnp.float32) ** shard_levels(streams_of[5], (RAY_TOTAL, DIRECTIONS, LATERAL_CELLS), ((0, 8),), -0.2, 0.2)), 0.0001, 0.004)
    ray_index = place_ends(jax.random.randint(streams_of[6], (CENTRES, FOOT_SLOTS), 0, RAY_ROWS), jax.random.fold_in(streams_of[6], 1), 0, RAY_ROWS - 1).astype(jnp.int32)
    foot_count = jax.vmap(lambda own: uneven_parts(own, CENTRE_DEV, LIVE_DEV, FOOT_SLOTS, 2))(jax.random.split(streams_of[7], GROUPS)).reshape((GROUPS, CENTRE_DEV)).astype(jnp.int32)
    foot_tiles = draw_foot_tiles(jax.random.fold_in(streams_of[10], 71), 0)
    tile_owner = draw_tile_owner(jax.random.fold_in(streams_of[10], 71), 0)
    return {"traces": traces, "send_table": send_table, "window_slots": window_slots, "ray_depth": ray_depth, "ray_lateral": ray_lateral, "ray_spread": ray_spread, "ray_index": ray_index, "foot_count": foot_count, "foot_tiles": foot_tiles, "tile_owner": tile_owner}


def slant_tables():
    freq_index = jnp.arange(FREQUENCIES, dtype=jnp.float32)
    angular = 2.0 * math.pi * (4.0 + 60.0 * freq_index / FREQUENCIES)
    centred = jnp.arange(WINDOW, dtype=jnp.float32) - 0.5 * (WINDOW - 1)
    taper_weight = jnp.exp(-(centred / (0.25 * WINDOW)) ** 2) / math.sqrt(WINDOW)
    slowness = 2e-05 * (jnp.arange(DIRECTIONS, dtype=jnp.float32) - 0.5 * (DIRECTIONS - 1))
    stack_angle = angular[:, None, None] * slowness[None, :, None] * (25.0 * centred)[None, None, :]
    stack_real = (taper_weight * jnp.cos(stack_angle)).astype(jnp.bfloat16)
    stack_imag = (-taper_weight * jnp.sin(stack_angle)).astype(jnp.bfloat16)
    return (angular, stack_real, stack_imag)

def pair_factors(beam_real, beam_imag, depth_times, lateral_times, spread_rates, live_mask, angular):
    direction_count = beam_real.shape[1]
    freq_count = beam_real.shape[2]
    pair_count = depth_times.shape[0]
    weight_scale = (live_mask / math.sqrt(direction_count * freq_count))[:, None, None, None]
    depth_phase = angular[None, None, :, None] * depth_times[:, :, None, :]
    depth_cos = jnp.cos(depth_phase)
    depth_sin = jnp.sin(depth_phase)
    part_real = (beam_real[..., None] * depth_cos - beam_imag[..., None] * depth_sin) * weight_scale
    part_imag = (beam_real[..., None] * depth_sin + beam_imag[..., None] * depth_cos) * weight_scale
    depth_factor = jnp.stack([part_real, -part_imag], axis=1).astype(jnp.bfloat16)
    lateral_phase = angular[None, None, :, None] * lateral_times[:, :, None, :]
    damping = jnp.exp(-angular[None, None, :, None] * spread_rates[:, :, None, :])
    lateral_factor = jnp.stack([damping * jnp.cos(lateral_phase), damping * jnp.sin(lateral_phase)], axis=1).astype(jnp.bfloat16)
    depth_factor = depth_factor.reshape(pair_count, 2 * direction_count * freq_count, depth_times.shape[2])
    lateral_factor = lateral_factor.reshape(pair_count, 2 * direction_count * freq_count, lateral_times.shape[2])
    return (depth_factor, lateral_factor)

def reference(traces, send_table, window_slots, ray_depth, ray_lateral, ray_spread, ray_index, foot_count, foot_tiles, tile_owner):
    angular, stack_real, stack_imag = slant_tables()
    stack_real_wide = stack_real.astype(jnp.float32)
    stack_imag_wide = stack_imag.astype(jnp.float32)
    entries = CENTRE_DEV * FOOT_SLOTS
    entry_ids = jnp.arange(entries, dtype=jnp.int32)
    centre_local = entry_ids // FOOT_SLOTS
    slot_local = entry_ids % FOOT_SLOTS
    highest = lax.Precision.HIGHEST
    image_start = jnp.zeros((IMAGE_TILES, DEPTH_CELLS, LATERAL_CELLS), jnp.float32)

    def one_group(image_sum, flat_id):
        shot_id = flat_id // GROUPS
        group_id = flat_id % GROUPS
        slot_table = lax.dynamic_slice_in_dim(window_slots[shot_id], group_id * CENTRE_DEV, CENTRE_DEV, 0)
        source = slot_table // CAPACITY
        within = slot_table % CAPACITY
        local_rows = send_table[shot_id][source, group_id, within]
        trace_ids = source * TRACE_DEV + local_rows
        gathered = traces[shot_id][trace_ids]
        trace_real = gathered[..., :FREQUENCIES].astype(jnp.float32)
        trace_imag = gathered[..., FREQUENCIES:].astype(jnp.float32)
        beam_real = jnp.einsum('fpk,ckf->cpf', stack_real_wide, trace_real, precision=highest) - jnp.einsum('fpk,ckf->cpf', stack_imag_wide, trace_imag, precision=highest)
        beam_imag = jnp.einsum('fpk,ckf->cpf', stack_real_wide, trace_imag, precision=highest) + jnp.einsum('fpk,ckf->cpf', stack_imag_wide, trace_real, precision=highest)
        counts = foot_count[group_id]
        live_mask = (slot_local < counts[centre_local]).astype(jnp.float32)
        centre_rows = group_id * CENTRE_DEV + centre_local
        ray_rows = group_id * RAY_ROWS + ray_index[centre_rows, slot_local]
        tile_ids = foot_tiles[centre_rows, slot_local]
        depth_table = ray_depth[shot_id]

        def one_block(block_sum, block_id):
            chosen = lax.dynamic_slice_in_dim(entry_ids, block_id * 8, 8, 0)
            centres = centre_local[chosen]
            rows_now = ray_rows[chosen]
            depth_factor, lateral_factor = pair_factors(beam_real[centres], beam_imag[centres], depth_table[rows_now], ray_lateral[rows_now], ray_spread[rows_now], live_mask[chosen], angular)
            contribution = jnp.einsum('brz,brx->bzx', depth_factor.astype(jnp.float32), lateral_factor.astype(jnp.float32), precision=highest)
            return (block_sum.at[tile_ids[chosen]].add(contribution), None)
        image_sum, _ = lax.scan(one_block, image_sum, jnp.arange(entries // 8, dtype=jnp.int32))
        return (image_sum, None)
    image_full, _ = lax.scan(one_group, image_start, jnp.arange(SHOT_GATHERS * GROUPS, dtype=jnp.int32))
    tile_order = jnp.argsort(tile_owner, stable=True)
    return image_full[tile_order]
```

```python
import math

import jax
import jax.numpy as jnp
import numpy as np
from jax import lax
from jax.experimental import pallas as pl
from jax.experimental.pallas import tpu as pltpu
from jax.sharding import PartitionSpec as P

FREQUENCIES = 64
DIRECTIONS = 32
WINDOW = 32
LANES = 128
FIRST_HZ = 4.0
STEP_HZ = 60.0 / FREQUENCIES
SPANS = LANES // DIRECTIONS
STEPS = FREQUENCIES // SPANS
PARTS = 2
BLOCK = PARTS * LANES
CHUNKS = 8
CHUNK_STEPS = STEPS // CHUNKS
ROWS = 16


def fit_half_turn():
    nodes = 0.5 * np.cos((np.arange(400) + 0.5) * np.pi / 800)
    u = nodes * nodes
    sine = np.polynomial.polynomial.polyfit(u, np.sin(np.pi * nodes) / nodes, 5)
    cosine = np.polynomial.polynomial.polyfit(u, np.cos(np.pi * nodes), 6)
    return [float(v) for v in sine], [float(v) for v in cosine]


SINE, COSINE = fit_half_turn()


def horner(coefficients, u):
    total = coefficients[-1]
    for value in coefficients[-2::-1]:
        total = total * u + value
    return total


def turn(t):
    r = t - jnp.floor(t + 0.5)
    u = r * r
    s = r * horner(SINE, u)
    c = horner(COSINE, u)
    return 1.0 - 2.0 * (s * s), 2.0 * (s * c)


def stack_tables():
    freq = np.arange(FREQUENCIES, dtype=np.float32)
    angular = (2.0 * math.pi * (4.0 + 60.0 * freq / FREQUENCIES)).astype(np.float32)
    centred = (np.arange(WINDOW) - 0.5 * (WINDOW - 1)).astype(np.float32)
    taper = (np.exp(-((centred / (0.25 * WINDOW)) ** 2)) / math.sqrt(WINDOW)).astype(np.float32)
    slowness = (2e-05 * (np.arange(DIRECTIONS) - 0.5 * (DIRECTIONS - 1))).astype(np.float32)
    angle = angular[:, None, None] * slowness[None, :, None] * (25.0 * centred)[None, None, :]
    angle = angle.astype(np.float32)
    real = (taper * np.cos(angle)).astype(jnp.bfloat16).astype(np.float32)
    imag = (-taper * np.sin(angle)).astype(jnp.bfloat16).astype(np.float32)

    def lay(table):
        table = table.reshape(SPANS, STEPS, DIRECTIONS, WINDOW).transpose(1, 3, 0, 2)
        return np.ascontiguousarray(table.reshape(STEPS, WINDOW, LANES))

    return lay(real), lay(imag)


def beam_kernel(win_ref, real_ref, imag_ref, out_ref):
    centres = out_ref.shape[0]
    scale = 1.0 / math.sqrt(DIRECTIONS * FREQUENCIES)
    row = lax.broadcasted_iota(jnp.int32, (PARTS * FREQUENCIES, BLOCK), 0)
    col = lax.broadcasted_iota(jnp.int32, (PARTS * FREQUENCIES, BLOCK), 1)
    home = lax.div(col, LANES) * FREQUENCIES + lax.div(lax.rem(col, LANES), DIRECTIONS) * STEPS
    for step in range(STEPS):
        pick = jnp.where(row == home + step, 1.0, 0.0).astype(jnp.bfloat16)
        spread = jnp.dot(win_ref[...], pick, preferred_element_type=jnp.float32)
        real = jnp.zeros((centres, LANES), jnp.float32)
        imag = jnp.zeros((centres, LANES), jnp.float32)
        for k in range(WINDOW):
            tr = spread[k * centres : (k + 1) * centres, :LANES]
            ti = spread[k * centres : (k + 1) * centres, LANES:]
            sr = real_ref[step, k : k + 1, :]
            si = imag_ref[step, k : k + 1, :]
            real = real + (sr * tr - si * ti)
            imag = imag + (sr * ti + si * tr)
        out_ref[:, 2 * step, :] = real * scale
        out_ref[:, 2 * step + 1, :] = imag * scale


def beams(windows, centres):
    real, imag = stack_tables()
    return pl.pallas_call(
        beam_kernel,
        out_shape=jax.ShapeDtypeStruct((centres, PARTS * STEPS, LANES), jnp.float32),
        name="beams",
    )(windows, real, imag)


def start_phases(times, start_ref, shot):
    c, s = turn(FIRST_HZ * times)
    step_c, step_s = turn(STEP_HZ * times)
    span_c, span_s = turn((STEP_HZ * STEPS) * times)
    cs, ss = [c], [s]
    for _ in range(SPANS - 1):
        c, s = c * span_c - s * span_s, c * span_s + s * span_c
        cs.append(c)
        ss.append(s)
    start_ref[shot, 0] = jnp.concatenate(cs, axis=0).T
    start_ref[shot, 1] = jnp.concatenate(ss, axis=0).T
    start_ref[shot, 2] = jnp.concatenate([step_c] * SPANS, axis=0).T
    start_ref[shot, 3] = jnp.concatenate([step_s] * SPANS, axis=0).T


def start_lateral(lateral, spread, side_ref):
    def factor(hz):
        damping = jnp.exp((-2.0 * math.pi * hz) * spread)
        c, s = turn(hz * lateral)
        return damping * c, -(damping * s)

    re, im = factor(FIRST_HZ)
    side_ref[SPANS, 0], side_ref[SPANS, 1] = factor(STEP_HZ)
    span_re, span_im = factor(STEP_HZ * STEPS)
    for span in range(SPANS):
        side_ref[span, 0], side_ref[span, 1] = re, im
        re, im = re * span_re - im * span_im, re * span_im + im * span_re


def depth_chunk(chunk, centre, beam_ref, start_ref, state_ref, factor_ref):
    cells = start_ref.shape[2]
    for block in range(cells // ROWS):
        rows = pl.ds(block * ROWS, ROWS)
        state = []
        for shot in range(2):
            if chunk == 0:
                c0 = start_ref[shot, 0, rows, :]
                s0 = start_ref[shot, 1, rows, :]
                sc = start_ref[shot, 2, rows, :]
                ss = start_ref[shot, 3, rows, :]
                c1, s1 = c0 * sc - s0 * ss, s0 * sc + c0 * ss
                twice = 2.0 * sc
                state_ref[shot, 4, rows, :] = twice
            else:
                c0, s0, c1, s1, twice = [state_ref[shot, n, rows, :] for n in range(5)]
            state.append((c0, s0, c1, s1, twice))
        for inner in range(CHUNK_STEPS):
            step = chunk * CHUNK_STEPS + inner
            re = im = None
            for shot in range(2):
                c0, s0, c1, s1, twice = state[shot]
                br = beam_ref[shot, centre, 2 * step : 2 * step + 1, :]
                bi = beam_ref[shot, centre, 2 * step + 1 : 2 * step + 2, :]
                part_re = br * c0 - bi * s0
                part_im = br * s0 + bi * c0
                re = part_re if re is None else re + part_re
                im = part_im if im is None else im + part_im
                state[shot] = (c1, s1, twice * c1 - c0, twice * s1 - s0, twice)
            col = inner * BLOCK
            factor_ref[rows, col : col + LANES] = re.astype(jnp.bfloat16)
            factor_ref[rows, col + LANES : col + BLOCK] = im.astype(jnp.bfloat16)
        if chunk + 1 < CHUNKS:
            for shot in range(2):
                for n in range(4):
                    state_ref[shot, n, rows, :] = state[shot][n]


def lateral_chunk(chunk, side_ref, chain_ref, factor_ref):
    source = side_ref if chunk == 0 else chain_ref
    step_re, step_im = side_ref[SPANS, 0], side_ref[SPANS, 1]
    if chunk == 0:
        chain_ref[SPANS, 0], chain_ref[SPANS, 1] = step_re, step_im
    else:
        step_re, step_im = chain_ref[SPANS, 0], chain_ref[SPANS, 1]
    for span in range(SPANS):
        re, im = source[span, 0], source[span, 1]
        for inner in range(CHUNK_STEPS):
            at = inner * BLOCK + span * DIRECTIONS
            factor_ref[at : at + DIRECTIONS, :] = re.astype(jnp.bfloat16)
            factor_ref[at + LANES : at + LANES + DIRECTIONS, :] = im.astype(jnp.bfloat16)
            if chunk * CHUNK_STEPS + inner + 1 < STEPS:
                re, im = re * step_re - im * step_im, re * step_im + im * step_re
        if chunk + 1 < CHUNKS:
            chain_ref[span, 0], chain_ref[span, 1] = re, im


def one_entry(
    centre, tile, next_ref, beam_ref, out_ref, start_ref, state_ref, side_ref, chain_ref,
    depth_factors, lateral_factors,
):
    total = None
    for chunk in range(CHUNKS):
        depth_ref, lateral_ref = depth_factors[chunk % 2], lateral_factors[chunk % 2]
        depth_chunk(chunk, centre, beam_ref, start_ref, state_ref, depth_ref)
        lateral_chunk(chunk, side_ref, chain_ref, lateral_ref)
        if chunk < 2:
            start_phases(next_ref[chunk], start_ref, chunk)
        if chunk == 2:
            start_lateral(next_ref[2], next_ref[3], side_ref)
        part = jnp.dot(depth_ref[...], lateral_ref[...], preferred_element_type=jnp.float32)
        total = part if total is None else total + part
    out_ref[tile] = out_ref[tile] + total


def tile_kernel(
    meta_ref, rows_ref, centre_ref, tile_ref, beam_ref, own_ref, other_ref, lateral_ref, spread_ref,
    out_ref, start_ref, state_ref, side_ref, chain_ref, depth_even, depth_odd, lateral_even,
    lateral_odd, times_ref, sems,
):
    base, count = meta_ref[0], meta_ref[1]

    def times(n, slot):
        row = rows_ref[base + n]
        return [
            pltpu.make_async_copy(table.at[row], times_ref.at[slot, kind], sems.at[slot, kind])
            for kind, table in enumerate((own_ref, other_ref, lateral_ref, spread_ref))
        ]

    def fetch(n, slot):
        @pl.when(n < count)
        def _():
            for copy in times(n, slot):
                copy.start()

    def arrive(n, slot):
        @pl.when(n < count)
        def _():
            for copy in times(n, slot):
                copy.wait()

    fetch(0, 0)
    fetch(1, 1)
    out_ref[...] = jnp.zeros_like(out_ref)
    arrive(0, 0)

    @pl.when(count > 0)
    def _():
        for shot in range(2):
            start_phases(times_ref[0, shot], start_ref, shot)
        start_lateral(times_ref[0, 2], times_ref[0, 3], side_ref)

    def entry(n, carry):
        slot = lax.rem(n, 2)
        fetch(n + 2, slot)
        arrive(n + 1, 1 - slot)
        one_entry(
            centre_ref[base + n], tile_ref[base + n], times_ref.at[1 - slot], beam_ref, out_ref,
            start_ref, state_ref, side_ref, chain_ref, (depth_even, depth_odd),
            (lateral_even, lateral_odd),
        )
        return carry

    lax.fori_loop(0, count, entry, 0)


def tiles_of(meta, rows, centres, places, beam, depth, other_depth, lateral, spread, tile_count):
    cells, across = depth.shape[2], lateral.shape[2]
    scalars = pl.BlockSpec(memory_space=pltpu.SMEM)
    inside = pl.BlockSpec(memory_space=pltpu.VMEM)
    outside = pl.BlockSpec(memory_space=pl.ANY)
    return pl.pallas_call(
        tile_kernel,
        in_specs=[scalars] * 4 + [inside] + [outside] * 4,
        out_specs=inside,
        scratch_shapes=[
            pltpu.VMEM((2, 4, cells, LANES), jnp.float32),
            pltpu.VMEM((2, 5, cells, LANES), jnp.float32),
            pltpu.VMEM((SPANS + 1, 2, DIRECTIONS, across), jnp.float32),
            pltpu.VMEM((SPANS + 1, 2, DIRECTIONS, across), jnp.float32),
            pltpu.VMEM((cells, CHUNK_STEPS * BLOCK), jnp.bfloat16),
            pltpu.VMEM((cells, CHUNK_STEPS * BLOCK), jnp.bfloat16),
            pltpu.VMEM((CHUNK_STEPS * BLOCK, across), jnp.bfloat16),
            pltpu.VMEM((CHUNK_STEPS * BLOCK, across), jnp.bfloat16),
            pltpu.VMEM((2, 4) + depth.shape[1:], jnp.float32),
            pltpu.SemaphoreType.DMA((2, 4)),
        ],
        out_shape=jax.ShapeDtypeStruct((tile_count, cells, across), jnp.float32),
        compiler_params=pltpu.CompilerParams(vmem_limit_bytes=40 << 20),
        name="tiles_of",
    )(meta, rows, centres, places, beam, depth, other_depth, lateral, spread)


def body(
    traces, send_table, window_slots, ray_depth, ray_lateral, ray_spread,
    ray_index, foot_count, foot_tiles, tile_owner,
):
    groups = lax.axis_size("beam")
    shots = lax.axis_size("shot")
    pairs = shots // 2
    group_id = lax.axis_index("beam")
    shot_id = lax.axis_index("shot")
    pair_id, side = shot_id // 2, shot_id % 2
    swap = [(n, n ^ 1) for n in range(shots)]
    i32 = jnp.int32

    own_depth = ray_depth[0]
    other_depth = lax.ppermute(own_depth, "shot", swap)

    my_routes = lax.dynamic_index_in_dim(send_table[0], group_id, 0, keepdims=False)
    sent = traces[0][my_routes]
    arrived = lax.all_to_all(sent, "beam", split_axis=0, concat_axis=0, tiled=True)
    arrived = arrived.reshape(-1, arrived.shape[-1])
    slot_table = window_slots[0]
    centre_count = slot_table.shape[0]
    windows = arrived[slot_table.T.reshape(-1)]
    beam = beams(windows, centre_count)
    beam = jnp.stack([beam, lax.ppermute(beam, "shot", swap)])

    foot_slots = ray_index.shape[1]
    entries = centre_count * foot_slots
    slots = (entries + 1) // 2
    ids = jnp.arange(entries, dtype=i32)
    live = (jnp.arange(foot_slots, dtype=i32)[None, :] < foot_count[0][:, None]).reshape(-1)
    my_tiles = lax.dynamic_slice_in_dim(
        foot_tiles, group_id * centre_count, centre_count, 0
    ).reshape(-1)
    owner = tile_owner[my_tiles]
    owner_shot, owner_group = owner // groups, owner % groups
    phase = (pair_id - owner_shot // 2 + pairs - 1) % pairs
    key = jnp.where(live, phase * entries + ids, pairs * entries)
    place = jnp.sum((key[None, :] < key[:, None]).astype(i32), axis=1)
    row = ray_index.reshape(-1)
    tile = ((owner_shot % 2) ^ side) * groups + owner_group
    numbers = jnp.stack([row, ids // foot_slots, tile])

    def listed(which):
        wanted = 2 * jnp.arange(slots, dtype=i32) + which
        chosen = live[None, :] & (place[None, :] == wanted[:, None])
        return jnp.sum(jnp.where(chosen[None], numbers[:, None, :], 0), axis=2)

    rows, centres, places = listed(side)
    ends = jnp.sum(
        (live[None, :] & (phase[None, :] <= jnp.arange(pairs, dtype=i32)[:, None])).astype(i32),
        axis=1,
    )
    ends = (ends - side + 1) // 2
    starts = jnp.concatenate([jnp.zeros((1,), i32), ends[:-1]])


    image = None
    for n in range(pairs):
        meta = jnp.stack([starts[n], ends[n] - starts[n]])
        part = tiles_of(
            meta, rows, centres, places, beam, own_depth, other_depth, ray_lateral, ray_spread,
            2 * groups,
        )
        part = part[:groups] + lax.ppermute(part[groups:], "shot", swap)
        if n + 1 < pairs:
            part = lax.ppermute(
                part,
                "shot",
                [(2 * q + c, 2 * ((q - n - 1) % pairs) + c) for q in range(pairs) for c in range(2)],
            )
        image = part if image is None else image + part
    received = lax.all_to_all(image, "beam", split_axis=0, concat_axis=0, tiled=True)

    tile_count = tile_owner.shape[0]
    tiles_each = tile_count // (shots * groups)
    numbers = jnp.arange(tile_count, dtype=i32)
    mine = tile_owner == shot_id * groups + group_id
    rank = jnp.sum((mine[None, :] & (numbers[None, :] < numbers[:, None])).astype(i32), axis=1)
    named = jnp.any(
        foot_tiles.reshape(groups, -1, 1) == numbers[None, None, :], axis=1
    )
    slot = jnp.sum(jnp.where(named & mine[None, :], rank[None, :], 0), axis=1)
    chosen = slot[None, :] == jnp.arange(tiles_each, dtype=i32)[:, None]
    return jnp.sum(jnp.where(chosen[:, :, None, None], received[None], 0.0), axis=1)


def solution(mesh):
    in_specs = (
        P("shot", "beam", None),
        P("shot", None, None, None),
        P("shot", "beam", None),
        P("shot", "beam", None, None),
        P("beam", None, None),
        P("beam", None, None),
        P("beam", None),
        P("beam", None),
        P(),
        P(),
    )
    out_specs = P(("shot", "beam"), None, None)
    return jax.shard_map(body, mesh=mesh, in_specs=in_specs, out_specs=out_specs, check_vma=False)
```

```python
import functools
import math

import jax
import jax.numpy as jnp
import numpy as np
from jax import lax
from jax.experimental import pallas as pl
from jax.experimental.pallas import tpu as pltpu
from jax.sharding import PartitionSpec as P

FREQUENCIES = 64
DIRECTIONS = 32
WINDOW = 32
LANES = 128
FIRST_HZ = 4.0
STEP_HZ = 60.0 / FREQUENCIES
SPANS = LANES // DIRECTIONS
STEPS = FREQUENCIES // SPANS
PARTS = 2
BLOCK = PARTS * LANES
CHUNKS = 8
CHUNK_STEPS = STEPS // CHUNKS
TIE = CHUNKS - 2
ROWS = 16


LONGEST = 0.25


def fit_half_turn(reach, sine_terms, cosine_terms):
    nodes = reach * np.cos((np.arange(400) + 0.5) * np.pi / 800)
    u = nodes * nodes
    sine = np.polynomial.polynomial.polyfit(u, np.sin(np.pi * nodes) / nodes, sine_terms - 1)
    cosine = np.polynomial.polynomial.polyfit(u, np.cos(np.pi * nodes), cosine_terms - 1)
    return [float(v) for v in sine], [float(v) for v in cosine]


WIDE = fit_half_turn(0.5, 5, 5)
NARROW = fit_half_turn(STEP_HZ * LONGEST, 4, 4)


def horner(coefficients, u):
    total = coefficients[-1]
    for value in coefficients[-2::-1]:
        total = total * u + value
    return total


def half_turn(r, fits):
    u = r * r
    return horner(fits[1], u), r * horner(fits[0], u)


def first_phase(times):
    c, s = half_turn(FIRST_HZ * times - 0.5, WIDE)
    twice = s + s
    return twice * s - 1.0, -(twice * c)


def step_phase(times):
    c, s = half_turn(STEP_HZ * times, NARROW)
    twice = s + s
    return 1.0 - twice * s, twice * c


def span_phase(c, s):
    for _ in range(STEPS.bit_length() - 1):
        twice = s + s
        c, s = 1.0 - twice * s, twice * c
    return c, s


def stack_tables():
    freq = np.arange(FREQUENCIES, dtype=np.float32)
    angular = (2.0 * math.pi * (4.0 + 60.0 * freq / FREQUENCIES)).astype(np.float32)
    centred = (np.arange(WINDOW) - 0.5 * (WINDOW - 1)).astype(np.float32)
    taper = (np.exp(-((centred / (0.25 * WINDOW)) ** 2)) / math.sqrt(WINDOW)).astype(np.float32)
    slowness = (2e-05 * (np.arange(DIRECTIONS) - 0.5 * (DIRECTIONS - 1))).astype(np.float32)
    angle = angular[:, None, None] * slowness[None, :, None] * (25.0 * centred)[None, None, :]
    angle = angle.astype(np.float32)
    real = (taper * np.cos(angle)).astype(jnp.bfloat16).astype(np.float32)
    imag = (-taper * np.sin(angle)).astype(jnp.bfloat16).astype(np.float32)

    def lay(table):
        table = table.reshape(SPANS, STEPS, DIRECTIONS, WINDOW).transpose(1, 3, 0, 2)
        return np.ascontiguousarray(table.reshape(STEPS, WINDOW, LANES))

    return lay(real), lay(imag)


def pick_rows(table, held, across):
    outer, inner = table.shape
    count = outer * inner
    n = lax.broadcasted_iota(jnp.int32, (count, outer), 0)
    m = lax.broadcasted_iota(jnp.int32, (count, inner), 0)
    n, m = (lax.rem(n, outer), lax.div(m, outer)) if across else (lax.div(n, inner), lax.rem(m, inner))
    of_row = jnp.where(lax.broadcasted_iota(jnp.int32, (count, outer), 1) == n, 1.0, 0.0)
    spread = jnp.dot(
        of_row, table.astype(jnp.float32), precision=lax.Precision.HIGHEST,
        preferred_element_type=jnp.float32,
    )
    kept = jnp.where(lax.broadcasted_iota(jnp.int32, (count, inner), 1) == m, spread, 0.0)
    number = jnp.sum(kept, axis=1, keepdims=True).astype(jnp.int32)
    choice = lax.broadcasted_iota(jnp.int32, (count, held.shape[0]), 1) == number
    choice = jnp.where(choice, 1.0, 0.0).astype(jnp.bfloat16)
    return jnp.dot(choice, held, preferred_element_type=jnp.float32).astype(jnp.bfloat16)


def route_kernel(table_ref, held_ref, out_ref):
    table = table_ref[0, lax.axis_index("beam")]
    out_ref[...] = pick_rows(table, held_ref[0], False).reshape(out_ref.shape)


def routed(table, held):
    return pl.pallas_call(
        route_kernel,
        out_shape=jax.ShapeDtypeStruct(table.shape[2:] + held.shape[2:], held.dtype),
        name="routed",
    )(table, held)


def beam_kernel(slot_ref, arrived_ref, real_ref, imag_ref, out_ref):
    centres = out_ref.shape[0]
    windows = pick_rows(slot_ref[0], arrived_ref[...], True)
    scale = 1.0 / math.sqrt(DIRECTIONS * FREQUENCIES)
    row = lax.broadcasted_iota(jnp.int32, (PARTS * FREQUENCIES, BLOCK), 0)
    col = lax.broadcasted_iota(jnp.int32, (PARTS * FREQUENCIES, BLOCK), 1)
    home = lax.div(col, LANES) * FREQUENCIES + lax.div(lax.rem(col, LANES), DIRECTIONS) * STEPS
    for step in range(STEPS):
        pick = jnp.where(row == home + step, 1.0, 0.0).astype(jnp.bfloat16)
        spread = jnp.dot(windows, pick, preferred_element_type=jnp.float32)
        real = jnp.zeros((centres, LANES), jnp.float32)
        imag = jnp.zeros((centres, LANES), jnp.float32)
        for k in range(WINDOW):
            tr = spread[k * centres : (k + 1) * centres, :LANES]
            ti = spread[k * centres : (k + 1) * centres, LANES:]
            sr = real_ref[step, k : k + 1, :]
            si = imag_ref[step, k : k + 1, :]
            real = real + (sr * tr - si * ti)
            imag = imag + (sr * ti + si * tr)
        out_ref[:, 2 * step, :] = real * scale
        out_ref[:, 2 * step + 1, :] = imag * scale


def beams(slots, arrived, centres):
    real, imag = stack_tables()
    return pl.pallas_call(
        beam_kernel,
        out_shape=jax.ShapeDtypeStruct((centres, PARTS * STEPS, LANES), jnp.float32),
        name="beams",
    )(slots, arrived, real, imag)


def start_phases(times, start_ref, shot):
    c, s = first_phase(times)
    step_c, step_s = step_phase(times)
    span_c, span_s = span_phase(step_c, step_s)
    cs, ss = [c], [s]
    for _ in range(SPANS - 1):
        c, s = c * span_c - s * span_s, c * span_s + s * span_c
        cs.append(c)
        ss.append(s)
    mark = None
    for n, pieces in enumerate((cs, ss, [step_c] * SPANS, [step_s] * SPANS)):
        turned = jnp.concatenate(pieces, axis=0).T
        start_ref[shot, n] = turned
        last = turned[-ROWS:]
        mark = last if mark is None else mark + last
    return mark


def start_lateral(lateral, spread, side_ref):
    def damped(hz, phase):
        damping = jnp.exp((-2.0 * math.pi * hz) * spread)
        return damping * phase[0], -(damping * phase[1])

    re, im = damped(FIRST_HZ, first_phase(lateral))
    step_re, step_im = damped(STEP_HZ, step_phase(lateral))
    side_ref[SPANS, 0], side_ref[SPANS, 1] = step_re, step_im
    span_re, span_im = step_re, step_im
    for _ in range(STEPS.bit_length() - 1):
        span_re, span_im = span_re * span_re - span_im * span_im, 2.0 * (span_re * span_im)
    for span in range(SPANS):
        side_ref[span, 0], side_ref[span, 1] = re, im
        re, im = re * span_re - im * span_im, re * span_im + im * span_re


def depth_chunk(chunk, centre, beam_refs, start_ref, state_ref, factor_ref, marks):
    cells = start_ref.shape[2]
    for block in range(cells // ROWS):
        rows = pl.ds(block * ROWS, ROWS)
        state = []
        for shot in range(2):
            if chunk == 0:
                c0 = start_ref[shot, 0, rows, :]
                s0 = start_ref[shot, 1, rows, :]
                sc = start_ref[shot, 2, rows, :]
                ss = start_ref[shot, 3, rows, :]
                c1, s1 = c0 * sc - s0 * ss, s0 * sc + c0 * ss
                twice = 2.0 * sc
                state_ref[shot, 4, rows, :] = twice
            else:
                c0, s0, c1, s1, twice = [state_ref[shot, n, rows, :] for n in range(5)]
                if chunk == TIE and block == 0:
                    c0 = jnp.where(marks[shot] > 100.0, marks[shot], c0)
            state.append((c0, s0, c1, s1, twice))
        for inner in range(CHUNK_STEPS):
            step = chunk * CHUNK_STEPS + inner
            re = im = None
            for shot in range(2):
                c0, s0, c1, s1, twice = state[shot]
                br = beam_refs[shot][centre, 2 * step : 2 * step + 1, :]
                bi = beam_refs[shot][centre, 2 * step + 1 : 2 * step + 2, :]
                part_re = br * c0 - bi * s0
                part_im = br * s0 + bi * c0
                re = part_re if re is None else re + part_re
                im = part_im if im is None else im + part_im
                state[shot] = (c1, s1, twice * c1 - c0, twice * s1 - s0, twice)
            col = inner * BLOCK
            factor_ref[rows, col : col + LANES] = re.astype(jnp.bfloat16)
            factor_ref[rows, col + LANES : col + BLOCK] = im.astype(jnp.bfloat16)
        if chunk + 1 < CHUNKS:
            for shot in range(2):
                for n in range(4):
                    state_ref[shot, n, rows, :] = state[shot][n]


def lateral_chunk(chunk, side_ref, chain_ref, factor_ref):
    source = side_ref if chunk == 0 else chain_ref
    step_re, step_im = side_ref[SPANS, 0], side_ref[SPANS, 1]
    if chunk == 0:
        chain_ref[SPANS, 0], chain_ref[SPANS, 1] = step_re, step_im
    else:
        step_re, step_im = chain_ref[SPANS, 0], chain_ref[SPANS, 1]
    for span in range(SPANS):
        re, im = source[span, 0], source[span, 1]
        for inner in range(CHUNK_STEPS):
            at = inner * BLOCK + span * DIRECTIONS
            factor_ref[at : at + DIRECTIONS, :] = re.astype(jnp.bfloat16)
            factor_ref[at + LANES : at + LANES + DIRECTIONS, :] = im.astype(jnp.bfloat16)
            if chunk * CHUNK_STEPS + inner + 1 < STEPS:
                re, im = re * step_re - im * step_im, re * step_im + im * step_re
        if chunk + 1 < CHUNKS:
            chain_ref[span, 0], chain_ref[span, 1] = re, im


def product(chunk, depth_factors, lateral_factors):
    return jnp.dot(
        depth_factors[chunk % 2][...],
        lateral_factors[chunk % 2][...],
        preferred_element_type=jnp.float32,
    )


def one_entry(
    centre, tile, last_tile, next_ref, beam_refs, image_ref, start_ref, state_ref, side_ref,
    chain_ref, depth_factors, lateral_factors,
):
    total, marks = None, []
    for chunk in range(CHUNKS):
        part = product(chunk - 1, depth_factors, lateral_factors)
        if chunk == 0:
            image_ref[last_tile] = image_ref[last_tile] + part
        else:
            total = part if total is None else total + part
        depth_chunk(
            chunk, centre, beam_refs, start_ref, state_ref, depth_factors[chunk % 2], marks
        )
        lateral_chunk(chunk, side_ref, chain_ref, lateral_factors[chunk % 2])
        if chunk < 2:
            marks.append(start_phases(next_ref[chunk], start_ref, chunk))
        if chunk == 2:
            start_lateral(next_ref[2], next_ref[3], side_ref)
    image_ref[tile] = image_ref[tile] + total


def steps_on(entry, counts):
    centre, slot = entry
    return settle(centre, slot + 2, counts, 2)


def settle(centre, slot, counts, most):
    for _ in range(most):
        held = counts[0, jnp.minimum(centre, counts.shape[1] - 1)]
        over = slot >= held
        slot = jnp.where(over, slot - held, slot)
        centre = jnp.where(over, centre + 1, centre)
    return centre, slot


def ray_row(entry, index_ref):
    centres, slots = index_ref.shape
    return index_ref[jnp.minimum(entry[0], centres - 1), jnp.minimum(entry[1], slots - 1)]


def first_entry(counts):
    side = lax.rem(lax.axis_index("shot"), 2)
    return settle(jnp.int32(0), side, counts, 1)


def first_kernel(
    count_ref, index_ref, own_ref, other_ref, lateral_ref, spread_ref, start_ref, side_ref,
    times_ref, sems,
):
    row = ray_row(first_entry(count_ref), index_ref)
    copies = first_times(row, (own_ref, other_ref, lateral_ref, spread_ref), times_ref, sems)
    for copy in copies:
        copy.start()
    for copy in copies:
        copy.wait()
    for shot in range(2):
        start_phases(times_ref[shot], start_ref, shot)
    start_lateral(times_ref[2], times_ref[3], side_ref)


def first_times(row, tables, times_ref, sems):
    return [
        pltpu.make_async_copy(table.at[row], times_ref.at[kind], sems.at[kind])
        for kind, table in enumerate(tables)
    ]


def first_of(foot_count, ray_index, tables):
    cells, across = tables[0].shape[2], tables[2].shape[2]
    scalars = pl.BlockSpec(memory_space=pltpu.SMEM)
    inside = pl.BlockSpec(memory_space=pltpu.VMEM)
    outside = pl.BlockSpec(memory_space=pltpu.HBM)
    return pl.pallas_call(
        first_kernel,
        in_specs=[scalars] * 2 + [outside] * 4,
        out_specs=[inside, inside],
        scratch_shapes=[
            pltpu.VMEM((4,) + tables[0].shape[1:], jnp.float32),
            pltpu.SemaphoreType.DMA((4,)),
        ],
        out_shape=[
            jax.ShapeDtypeStruct((2, 4, cells, LANES), jnp.float32),
            jax.ShapeDtypeStruct((SPANS + 1, 2, DIRECTIONS, across), jnp.float32),
        ],
        name="first_of",
    )(foot_count, ray_index, *tables)


def tile_kernel(
    count_ref, index_ref, tiles_ref, owner_ref, first_start, first_side, own_beam, other_beam,
    own_ref, other_ref, lateral_ref, spread_ref, mine_ref, theirs_ref, image_ref, start_ref,
    state_ref, side_ref, chain_ref, depth_even, depth_odd, lateral_even, lateral_odd, times_ref,
    sems,
):
    group, side = lax.axis_index("beam"), lax.rem(lax.axis_index("shot"), 2)
    groups = lax.axis_size("beam")
    half = mine_ref.shape[0]
    centres = index_ref.shape[0]
    found = count_ref[0, 0]
    for n in range(1, centres):
        found = found + count_ref[0, n]
    count = lax.div(found - side + 1, 2)
    depth_factors, lateral_factors = (depth_even, depth_odd), (lateral_even, lateral_odd)
    tables = (own_ref, other_ref, lateral_ref, spread_ref)

    def times(entry, slot):
        return first_times(ray_row(entry, index_ref), tables, times_ref.at[slot], sems.at[slot])

    def fetch(entry, slot):
        for copy in times(entry, slot):
            copy.start()

    def arrive(entry, slot):
        for copy in times(entry, slot):
            copy.wait()

    def tile_of(entry):
        owner = owner_ref[tiles_ref[group * centres + entry[0], entry[1]]]
        shot, home = lax.div(owner, groups), lax.rem(owner, groups)
        away = jnp.where(lax.rem(shot, 2) == side, 0, half)
        return lax.div(shot, 2) * groups + home + away

    def one(n, carry):
        entry, later, last = carry
        slot = lax.rem(n, 2)
        after = steps_on(later, count_ref)
        arrive(later, 1 - slot)
        fetch(after, slot)
        tile = tile_of(entry)
        one_entry(
            entry[0], tile, last, times_ref.at[1 - slot], (own_beam, other_beam), image_ref,
            start_ref, state_ref, side_ref, chain_ref, depth_factors, lateral_factors,
        )
        return later, after, tile

    first = first_entry(count_ref)
    second = steps_on(first, count_ref)
    fetch(second, 1)
    image_ref[...] = jnp.zeros_like(image_ref)
    depth_odd[...] = jnp.zeros_like(depth_odd)
    lateral_odd[...] = jnp.zeros_like(lateral_odd)
    start_ref[...] = first_start[...]
    side_ref[...] = first_side[...]
    _, later, last = lax.fori_loop(0, count, one, (first, second, jnp.int32(0)))
    arrive(later, lax.rem(count + 1, 2))
    part = product(CHUNKS - 1, depth_factors, lateral_factors)
    image_ref[last] = image_ref[last] + part
    mine_ref[...] = image_ref[:half]
    theirs_ref[...] = image_ref[half:].astype(theirs_ref.dtype)


def tiles_of(entries, firsts, beams, tables, tiles):
    cells, across = tables[0].shape[2], tables[2].shape[2]
    scalars = pl.BlockSpec(memory_space=pltpu.SMEM)
    inside = pl.BlockSpec(memory_space=pltpu.VMEM)
    outside = pl.BlockSpec(memory_space=pltpu.HBM)
    return pl.pallas_call(
        tile_kernel,
        in_specs=[scalars] * 4 + [inside] * 4 + [outside] * 4,
        out_specs=[inside] * 2,
        scratch_shapes=[
            pltpu.VMEM((2 * tiles, cells, across), jnp.float32),
            pltpu.VMEM((2, 4, cells, LANES), jnp.float32),
            pltpu.VMEM((2, 5, cells, LANES), jnp.float32),
            pltpu.VMEM((SPANS + 1, 2, DIRECTIONS, across), jnp.float32),
            pltpu.VMEM((SPANS + 1, 2, DIRECTIONS, across), jnp.float32),
            pltpu.VMEM((cells, CHUNK_STEPS * BLOCK), jnp.bfloat16),
            pltpu.VMEM((cells, CHUNK_STEPS * BLOCK), jnp.bfloat16),
            pltpu.VMEM((CHUNK_STEPS * BLOCK, across), jnp.bfloat16),
            pltpu.VMEM((CHUNK_STEPS * BLOCK, across), jnp.bfloat16),
            pltpu.VMEM((2, 4) + tables[0].shape[1:], jnp.float32),
            pltpu.SemaphoreType.DMA((2, 4)),
        ],
        out_shape=[
            jax.ShapeDtypeStruct((tiles, cells, across), kind)
            for kind in (jnp.float32, jnp.bfloat16)
        ],
        compiler_params=pltpu.CompilerParams(vmem_limit_bytes=60 << 20),
        cost_estimate=pl.CostEstimate(
            flops=40_000_000_000, transcendentals=0, bytes_accessed=4_000_000
        ),
        name="tiles_of",
    )(*entries, *firsts, *beams, *tables)


def body(
    traces, send_table, window_slots, ray_depth, ray_lateral, ray_spread,
    ray_index, foot_count, foot_tiles, tile_owner,
):
    groups = lax.axis_size("beam")
    shots = lax.axis_size("shot")
    pairs = shots // 2
    group_id = lax.axis_index("beam")
    shot_id = lax.axis_index("shot")
    swap = [(n, n ^ 1) for n in range(shots)]
    i32 = jnp.int32

    own_depth = ray_depth[0]
    other_depth = lax.ppermute(own_depth, "shot", swap)

    sent = routed(send_table, traces)
    arrived = lax.all_to_all(sent, "beam", split_axis=0, concat_axis=0, tiled=True)
    arrived = arrived.reshape(-1, arrived.shape[-1])
    tables = (own_depth, other_depth, ray_lateral, ray_spread)
    firsts = first_of(foot_count, ray_index, tables)
    entries = (foot_count, ray_index, foot_tiles, tile_owner)
    arrived, firsts = lax.optimization_barrier((arrived, firsts))
    own_beam = beams(window_slots, arrived, window_slots.shape[1])
    other_beam = lax.ppermute(own_beam, "shot", swap)

    image, theirs = tiles_of(entries, firsts, (own_beam, other_beam), tables, pairs * groups)
    image = image + lax.ppermute(theirs, "shot", swap).astype(jnp.float32)
    same_side = [
        [(2 * q + c) * groups + n for q in range(pairs) for n in range(groups)] for c in range(2)
    ]
    received = lax.all_to_all(
        image.astype(jnp.bfloat16), ("shot", "beam"), split_axis=0, concat_axis=0, tiled=True,
        axis_index_groups=same_side,
    )

    tile_count = tile_owner.shape[0]
    tiles_each = tile_count // (shots * groups)
    numbers = jnp.arange(tile_count, dtype=i32)
    mine = tile_owner == shot_id * groups + group_id
    rank = jnp.sum((mine[None, :] & (numbers[None, :] < numbers[:, None])).astype(i32), axis=1)
    named = jnp.any(
        foot_tiles.reshape(groups, -1, 1) == numbers[None, None, :], axis=1
    )
    slot = jnp.sum(jnp.where(named & mine[None, :], rank[None, :], 0), axis=1)
    chosen = slot[None, :] == jnp.arange(tiles_each, dtype=i32)[:, None]
    received = received.reshape((pairs, groups) + received.shape[1:]).astype(jnp.float32)
    received = jnp.sum(received, axis=0)
    return jnp.sum(jnp.where(chosen[:, :, None, None], received[None], 0.0), axis=1)


def solution(mesh):
    in_specs = (
        P("shot", "beam", None),
        P("shot", None, None, None),
        P("shot", "beam", None),
        P("shot", "beam", None, None),
        P("beam", None, None),
        P("beam", None, None),
        P("beam", None),
        P("beam", None),
        P(),
        P(),
    )
    out_specs = P(("shot", "beam"), None, None)
    return jax.shard_map(body, mesh=mesh, in_specs=in_specs, out_specs=out_specs, check_vma=False)
```

```python
import functools
import math

import jax
import jax.numpy as jnp
import numpy as np
from jax import lax
from jax.experimental import pallas as pl
from jax.experimental.pallas import tpu as pltpu
from jax.sharding import PartitionSpec as P

FREQUENCIES = 64
DIRECTIONS = 32
WINDOW = 32
LANES = 128
FIRST_HZ = 4.0
STEP_HZ = 60.0 / FREQUENCIES
SPANS = LANES // DIRECTIONS
STEPS = FREQUENCIES // SPANS
PARTS = 2
BLOCK = PARTS * LANES
CHUNKS = 8
CHUNK_STEPS = STEPS // CHUNKS
TIE = CHUNKS - 2
ROWS = 16


LONGEST = 0.25


def fit_half_turn(reach, sine_terms, cosine_terms):
    nodes = reach * np.cos((np.arange(400) + 0.5) * np.pi / 800)
    u = nodes * nodes
    sine = np.polynomial.polynomial.polyfit(u, np.sin(np.pi * nodes) / nodes, sine_terms - 1)
    cosine = np.polynomial.polynomial.polyfit(u, np.cos(np.pi * nodes), cosine_terms - 1)
    return [float(v) for v in sine], [float(v) for v in cosine]


WIDE = fit_half_turn(0.5, 5, 5)
NARROW = fit_half_turn(STEP_HZ * LONGEST, 4, 4)


def horner(coefficients, u):
    total = coefficients[-1]
    for value in coefficients[-2::-1]:
        total = total * u + value
    return total


def half_turn(r, fits):
    u = r * r
    return horner(fits[1], u), r * horner(fits[0], u)


def first_phase(times):
    c, s = half_turn(FIRST_HZ * times - 0.5, WIDE)
    twice = s + s
    return twice * s - 1.0, -(twice * c)


def step_phase(times):
    c, s = half_turn(STEP_HZ * times, NARROW)
    twice = s + s
    return 1.0 - twice * s, twice * c


def span_phase(c, s):
    for _ in range(STEPS.bit_length() - 1):
        twice = s + s
        c, s = 1.0 - twice * s, twice * c
    return c, s


def stack_tables():
    freq = np.arange(FREQUENCIES, dtype=np.float32)
    angular = (2.0 * math.pi * (4.0 + 60.0 * freq / FREQUENCIES)).astype(np.float32)
    centred = (np.arange(WINDOW) - 0.5 * (WINDOW - 1)).astype(np.float32)
    taper = (np.exp(-((centred / (0.25 * WINDOW)) ** 2)) / math.sqrt(WINDOW)).astype(np.float32)
    slowness = (2e-05 * (np.arange(DIRECTIONS) - 0.5 * (DIRECTIONS - 1))).astype(np.float32)
    angle = angular[:, None, None] * slowness[None, :, None] * (25.0 * centred)[None, None, :]
    angle = angle.astype(np.float32)
    real = (taper * np.cos(angle)).astype(jnp.bfloat16).astype(np.float32)
    imag = (-taper * np.sin(angle)).astype(jnp.bfloat16).astype(np.float32)

    def lay(table):
        table = table.reshape(SPANS, STEPS, DIRECTIONS, WINDOW).transpose(1, 3, 0, 2)
        return np.ascontiguousarray(table.reshape(STEPS, WINDOW, LANES))

    return lay(real), lay(imag)


def pick_rows(table, held, across):
    outer, inner = table.shape
    count = outer * inner
    n = lax.broadcasted_iota(jnp.int32, (count, outer), 0)
    m = lax.broadcasted_iota(jnp.int32, (count, inner), 0)
    n, m = (lax.rem(n, outer), lax.div(m, outer)) if across else (lax.div(n, inner), lax.rem(m, inner))
    of_row = jnp.where(lax.broadcasted_iota(jnp.int32, (count, outer), 1) == n, 1.0, 0.0)
    halves = jnp.concatenate([lax.div(table, 256), lax.rem(table, 256)], axis=1)
    spread = jnp.dot(
        of_row.astype(jnp.bfloat16), halves.astype(jnp.float32).astype(jnp.bfloat16),
        preferred_element_type=jnp.float32,
    )
    spread = 256.0 * spread[:, :inner] + spread[:, inner:]
    kept = jnp.where(lax.broadcasted_iota(jnp.int32, (count, inner), 1) == m, spread, 0.0)
    number = jnp.sum(kept, axis=1, keepdims=True).astype(jnp.int32)
    choice = lax.broadcasted_iota(jnp.int32, (count, held.shape[0]), 1) == number
    choice = jnp.where(choice, 1.0, 0.0).astype(jnp.bfloat16)
    return jnp.dot(choice, held, preferred_element_type=jnp.float32).astype(jnp.bfloat16)


def route_kernel(table_ref, held_ref, out_ref):
    table = table_ref[0, lax.axis_index("beam")]
    out_ref[...] = pick_rows(table, held_ref[0], False).reshape(out_ref.shape)


def routed(table, held):
    return pl.pallas_call(
        route_kernel,
        out_shape=jax.ShapeDtypeStruct(table.shape[2:] + held.shape[2:], held.dtype),
        compiler_params=pltpu.CompilerParams(vmem_limit_bytes=61 << 20),
        name="routed",
    )(table, held)


def beam_kernel(slot_ref, arrived_ref, real_ref, imag_ref, out_ref):
    centres = out_ref.shape[0]
    windows = pick_rows(slot_ref[0], arrived_ref[...], True)
    scale = 1.0 / math.sqrt(DIRECTIONS * FREQUENCIES)
    row = lax.broadcasted_iota(jnp.int32, (PARTS * FREQUENCIES, BLOCK), 0)
    col = lax.broadcasted_iota(jnp.int32, (PARTS * FREQUENCIES, BLOCK), 1)
    home = lax.div(col, LANES) * FREQUENCIES + lax.div(lax.rem(col, LANES), DIRECTIONS) * STEPS
    for step in range(STEPS):
        pick = jnp.where(row == home + step, 1.0, 0.0).astype(jnp.bfloat16)
        spread = jnp.dot(windows, pick, preferred_element_type=jnp.float32)
        real = jnp.zeros((centres, LANES), jnp.float32)
        imag = jnp.zeros((centres, LANES), jnp.float32)
        for k in range(WINDOW):
            tr = spread[k * centres : (k + 1) * centres, :LANES]
            ti = spread[k * centres : (k + 1) * centres, LANES:]
            sr = real_ref[step, k : k + 1, :]
            si = imag_ref[step, k : k + 1, :]
            real = real + (sr * tr - si * ti)
            imag = imag + (sr * ti + si * tr)
        out_ref[:, 2 * step, :] = real * scale
        out_ref[:, 2 * step + 1, :] = imag * scale


def beams(slots, arrived, centres):
    real, imag = stack_tables()
    return pl.pallas_call(
        beam_kernel,
        out_shape=jax.ShapeDtypeStruct((centres, PARTS * STEPS, LANES), jnp.float32),
        compiler_params=pltpu.CompilerParams(vmem_limit_bytes=16 << 20),
        name="beams",
    )(slots, arrived, real, imag)


def start_phases(times, start_ref, shot):
    c, s = first_phase(times)
    step_c, step_s = step_phase(times)
    span_c, span_s = span_phase(step_c, step_s)
    cs, ss = [c], [s]
    for _ in range(SPANS - 1):
        c, s = c * span_c - s * span_s, c * span_s + s * span_c
        cs.append(c)
        ss.append(s)
    mark = None
    for n, pieces in enumerate((cs, ss, [step_c] * SPANS, [step_s] * SPANS)):
        turned = jnp.concatenate(pieces, axis=0).T
        start_ref[shot, n] = turned
        last = turned[-ROWS:]
        mark = last if mark is None else mark + last
    return mark


def start_lateral(lateral, spread, side_ref):
    def damped(hz, phase):
        damping = jnp.exp((-2.0 * math.pi * hz) * spread)
        return damping * phase[0], -(damping * phase[1])

    re, im = damped(FIRST_HZ, first_phase(lateral))
    step_re, step_im = damped(STEP_HZ, step_phase(lateral))
    side_ref[SPANS, 0], side_ref[SPANS, 1] = step_re, step_im
    span_re, span_im = step_re, step_im
    for _ in range(STEPS.bit_length() - 1):
        span_re, span_im = span_re * span_re - span_im * span_im, 2.0 * (span_re * span_im)
    for span in range(SPANS):
        side_ref[span, 0], side_ref[span, 1] = re, im
        re, im = re * span_re - im * span_im, re * span_im + im * span_re


def depth_chunk(chunk, centre, beam_refs, start_ref, state_ref, factor_ref, marks):
    cells = start_ref.shape[2]
    for block in range(cells // ROWS):
        rows = pl.ds(block * ROWS, ROWS)
        state = []
        for shot in range(2):
            if chunk == 0:
                c0 = start_ref[shot, 0, rows, :]
                s0 = start_ref[shot, 1, rows, :]
                sc = start_ref[shot, 2, rows, :]
                ss = start_ref[shot, 3, rows, :]
                c1, s1 = c0 * sc - s0 * ss, s0 * sc + c0 * ss
                twice = 2.0 * sc
                state_ref[shot, 4, rows, :] = twice
            else:
                c0, s0, c1, s1, twice = [state_ref[shot, n, rows, :] for n in range(5)]
                if chunk == TIE and block == 0:
                    c0 = jnp.where(marks[shot] > 100.0, marks[shot], c0)
            state.append((c0, s0, c1, s1, twice))
        for inner in range(CHUNK_STEPS):
            step = chunk * CHUNK_STEPS + inner
            re = im = None
            for shot in range(2):
                c0, s0, c1, s1, twice = state[shot]
                br = beam_refs[shot][centre, 2 * step : 2 * step + 1, :]
                bi = beam_refs[shot][centre, 2 * step + 1 : 2 * step + 2, :]
                part_re = br * c0 - bi * s0
                part_im = br * s0 + bi * c0
                re = part_re if re is None else re + part_re
                im = part_im if im is None else im + part_im
                state[shot] = (c1, s1, twice * c1 - c0, twice * s1 - s0, twice)
            col = inner * BLOCK
            factor_ref[rows, col : col + LANES] = re.astype(jnp.bfloat16)
            factor_ref[rows, col + LANES : col + BLOCK] = im.astype(jnp.bfloat16)
        if chunk + 1 < CHUNKS:
            for shot in range(2):
                for n in range(4):
                    state_ref[shot, n, rows, :] = state[shot][n]


def lateral_chunk(chunk, side_ref, chain_ref, factor_ref):
    source = side_ref if chunk == 0 else chain_ref
    step_re, step_im = side_ref[SPANS, 0], side_ref[SPANS, 1]
    if chunk == 0:
        chain_ref[SPANS, 0], chain_ref[SPANS, 1] = step_re, step_im
    else:
        step_re, step_im = chain_ref[SPANS, 0], chain_ref[SPANS, 1]
    for span in range(SPANS):
        re, im = source[span, 0], source[span, 1]
        for inner in range(CHUNK_STEPS):
            at = inner * BLOCK + span * DIRECTIONS
            factor_ref[at : at + DIRECTIONS, :] = re.astype(jnp.bfloat16)
            factor_ref[at + LANES : at + LANES + DIRECTIONS, :] = im.astype(jnp.bfloat16)
            if chunk * CHUNK_STEPS + inner + 1 < STEPS:
                re, im = re * step_re - im * step_im, re * step_im + im * step_re
        if chunk + 1 < CHUNKS:
            chain_ref[span, 0], chain_ref[span, 1] = re, im


def product(chunk, depth_factors, lateral_factors):
    return jnp.dot(
        depth_factors[chunk % 2][...],
        lateral_factors[chunk % 2][...],
        preferred_element_type=jnp.float32,
    )


def one_entry(
    centre, tile, last_tile, next_ref, beam_refs, image_ref, start_ref, state_ref, side_ref,
    chain_ref, depth_factors, lateral_factors,
):
    total, marks = None, []
    for chunk in range(CHUNKS):
        part = product(chunk - 1, depth_factors, lateral_factors)
        if chunk == 0:
            image_ref[last_tile] = image_ref[last_tile] + part
        else:
            total = part if total is None else total + part
        depth_chunk(
            chunk, centre, beam_refs, start_ref, state_ref, depth_factors[chunk % 2], marks
        )
        lateral_chunk(chunk, side_ref, chain_ref, lateral_factors[chunk % 2])
        if chunk < 2:
            marks.append(start_phases(next_ref[chunk], start_ref, chunk))
        if chunk == 2:
            start_lateral(next_ref[2], next_ref[3], side_ref)
    image_ref[tile] = image_ref[tile] + total


def steps_on(entry, counts):
    centre, slot = entry
    return settle(centre, slot + 2, counts, 2)


def settle(centre, slot, counts, most):
    for _ in range(most):
        held = counts[0, jnp.minimum(centre, counts.shape[1] - 1)]
        over = slot >= held
        slot = jnp.where(over, slot - held, slot)
        centre = jnp.where(over, centre + 1, centre)
    return centre, slot


def ray_row(entry, index_ref):
    centres, slots = index_ref.shape
    return index_ref[jnp.minimum(entry[0], centres - 1), jnp.minimum(entry[1], slots - 1)]


def first_entry(counts):
    side = lax.rem(lax.axis_index("shot"), 2)
    return settle(jnp.int32(0), side, counts, 1)


def first_kernel(
    count_ref, index_ref, own_ref, other_ref, lateral_ref, spread_ref, start_ref, side_ref,
    times_ref, sems,
):
    row = ray_row(first_entry(count_ref), index_ref)
    copies = first_times(row, (own_ref, other_ref, lateral_ref, spread_ref), times_ref, sems)
    for copy in copies:
        copy.start()
    for copy in copies:
        copy.wait()
    for shot in range(2):
        start_phases(times_ref[shot], start_ref, shot)
    start_lateral(times_ref[2], times_ref[3], side_ref)


def first_times(row, tables, times_ref, sems):
    return [
        pltpu.make_async_copy(table.at[row], times_ref.at[kind], sems.at[kind])
        for kind, table in enumerate(tables)
    ]


def first_of(foot_count, ray_index, tables):
    cells, across = tables[0].shape[2], tables[2].shape[2]
    scalars = pl.BlockSpec(memory_space=pltpu.SMEM)
    inside = pl.BlockSpec(memory_space=pltpu.VMEM)
    outside = pl.BlockSpec(memory_space=pltpu.HBM)
    anywhere = pl.BlockSpec(memory_space=pl.ANY)
    return pl.pallas_call(
        first_kernel,
        in_specs=[scalars] * 2 + [outside, anywhere, outside, outside],
        out_specs=[inside, inside],
        scratch_shapes=[
            pltpu.VMEM((4,) + tables[0].shape[1:], jnp.float32),
            pltpu.SemaphoreType.DMA((4,)),
        ],
        out_shape=[
            jax.ShapeDtypeStruct((2, 4, cells, LANES), jnp.float32),
            jax.ShapeDtypeStruct((SPANS + 1, 2, DIRECTIONS, across), jnp.float32),
        ],
        compiler_params=pltpu.CompilerParams(vmem_limit_bytes=61 << 20),
        name="first_of",
    )(foot_count, ray_index, *tables)


def tile_kernel(
    count_ref, index_ref, tiles_ref, owner_ref, first_start, first_side, own_beam, other_beam,
    own_ref, other_ref, lateral_ref, spread_ref, mine_ref, theirs_ref, image_ref, start_ref,
    state_ref, side_ref, chain_ref, depth_even, depth_odd, lateral_even, lateral_odd, times_ref,
    beams_ref, sems, first_sems,
):
    group, side = lax.axis_index("beam"), lax.rem(lax.axis_index("shot"), 2)
    groups = lax.axis_size("beam")
    half = mine_ref.shape[0]
    centres = index_ref.shape[0]
    found = count_ref[0, 0]
    for n in range(1, centres):
        found = found + count_ref[0, n]
    count = lax.div(found - side + 1, 2)
    depth_factors, lateral_factors = (depth_even, depth_odd), (lateral_even, lateral_odd)
    tables = (own_ref, other_ref, lateral_ref, spread_ref)

    def times(entry, slot):
        return first_times(ray_row(entry, index_ref), tables, times_ref.at[slot], sems.at[slot])

    def fetch(entry, slot):
        for copy in times(entry, slot):
            copy.start()

    def arrive(entry, slot):
        for copy in times(entry, slot):
            copy.wait()

    def tile_of(entry):
        owner = owner_ref[tiles_ref[group * centres + entry[0], entry[1]]]
        shot, home = lax.div(owner, groups), lax.rem(owner, groups)
        away = jnp.where(lax.rem(shot, 2) == side, 0, half)
        return lax.div(shot, 2) * groups + home + away

    def one(n, carry):
        entry, later, last = carry
        slot = lax.rem(n, 2)
        after = steps_on(later, count_ref)
        arrive(later, 1 - slot)
        fetch(after, slot)
        tile = tile_of(entry)
        one_entry(
            entry[0], tile, last, times_ref.at[1 - slot], (beams_ref.at[0], beams_ref.at[1]), image_ref,
            start_ref, state_ref, side_ref, chain_ref, depth_factors, lateral_factors,
        )
        return later, after, tile

    first = first_entry(count_ref)
    second = steps_on(first, count_ref)
    fetch(second, 1)
    arriving = [
        pltpu.make_async_copy(source, target, first_sems.at[n])
        for n, (source, target) in enumerate(
            (
                (own_beam, beams_ref.at[0]), (other_beam, beams_ref.at[1]),
                (first_start, start_ref), (first_side, side_ref),
            )
        )
    ]
    for copy in arriving:
        copy.start()
    image_ref[...] = jnp.zeros_like(image_ref)
    depth_odd[...] = jnp.zeros_like(depth_odd)
    lateral_odd[...] = jnp.zeros_like(lateral_odd)
    for copy in arriving:
        copy.wait()
    _, later, last = lax.fori_loop(0, count, one, (first, second, jnp.int32(0)))
    arrive(later, lax.rem(count + 1, 2))
    part = product(CHUNKS - 1, depth_factors, lateral_factors)
    image_ref[last] = image_ref[last] + part
    mine_ref[...] = image_ref[:half].astype(mine_ref.dtype)
    theirs_ref[...] = image_ref[half:].astype(theirs_ref.dtype)


def tiles_of(entries, firsts, beams, tables, tiles):
    cells, across = tables[0].shape[2], tables[2].shape[2]
    scalars = pl.BlockSpec(memory_space=pltpu.SMEM)
    inside = pl.BlockSpec(memory_space=pltpu.VMEM)
    outside = pl.BlockSpec(memory_space=pltpu.HBM)
    anywhere = pl.BlockSpec(memory_space=pl.ANY)
    return pl.pallas_call(
        tile_kernel,
        in_specs=[scalars] * 4 + [anywhere] * 4 + [outside, anywhere, outside, outside],
        out_specs=[inside] * 2,
        scratch_shapes=[
            pltpu.VMEM((2 * tiles, cells, across), jnp.float32),
            pltpu.VMEM((2, 4, cells, LANES), jnp.float32),
            pltpu.VMEM((2, 5, cells, LANES), jnp.float32),
            pltpu.VMEM((SPANS + 1, 2, DIRECTIONS, across), jnp.float32),
            pltpu.VMEM((SPANS + 1, 2, DIRECTIONS, across), jnp.float32),
            pltpu.VMEM((cells, CHUNK_STEPS * BLOCK), jnp.bfloat16),
            pltpu.VMEM((cells, CHUNK_STEPS * BLOCK), jnp.bfloat16),
            pltpu.VMEM((CHUNK_STEPS * BLOCK, across), jnp.bfloat16),
            pltpu.VMEM((CHUNK_STEPS * BLOCK, across), jnp.bfloat16),
            pltpu.VMEM((2, 4) + tables[0].shape[1:], jnp.float32),
            pltpu.VMEM((2,) + beams[0].shape, jnp.float32),
            pltpu.SemaphoreType.DMA((2, 4)),
            pltpu.SemaphoreType.DMA((4,)),
        ],
        out_shape=[
            jax.ShapeDtypeStruct((tiles, cells, across), kind)
            for kind in (jnp.bfloat16, jnp.bfloat16)
        ],
        compiler_params=pltpu.CompilerParams(vmem_limit_bytes=61 << 20),
        cost_estimate=pl.CostEstimate(
            flops=40_000_000_000, transcendentals=0, bytes_accessed=4_000_000
        ),
        name="tiles_of",
    )(*entries, *firsts, *beams, *tables)


def add_kernel(one_ref, other_ref, out_ref):
    total = one_ref[...].astype(jnp.float32) + other_ref[...].astype(jnp.float32)
    out_ref[...] = total.astype(out_ref.dtype)


def added(one, other):
    return pl.pallas_call(
        add_kernel,
        out_shape=jax.ShapeDtypeStruct(one.shape, one.dtype),
        compiler_params=pltpu.CompilerParams(vmem_limit_bytes=16 << 20),
        name="added",
    )(one, other)


def body(
    traces, send_table, window_slots, ray_depth, ray_lateral, ray_spread,
    ray_index, foot_count, foot_tiles, tile_owner,
):
    groups = lax.axis_size("beam")
    shots = lax.axis_size("shot")
    pairs = shots // 2
    group_id = lax.axis_index("beam")
    shot_id = lax.axis_index("shot")
    swap = [(n, n ^ 1) for n in range(shots)]
    i32 = jnp.int32

    own_depth = ray_depth[0]
    other_depth = lax.ppermute(own_depth, "shot", swap)

    sent = routed(send_table, traces)
    arrived = lax.all_to_all(sent, "beam", split_axis=0, concat_axis=0, tiled=True)
    arrived = arrived.reshape(-1, arrived.shape[-1])
    tables = (own_depth, other_depth, ray_lateral, ray_spread)
    firsts = first_of(foot_count, ray_index, tables)
    entries = (foot_count, ray_index, foot_tiles, tile_owner)
    arrived, firsts = lax.optimization_barrier((arrived, firsts))
    own_beam = beams(window_slots, arrived, window_slots.shape[1])
    other_beam = lax.ppermute(own_beam, "shot", swap)

    image, theirs = tiles_of(entries, firsts, (own_beam, other_beam), tables, pairs * groups)
    theirs = lax.ppermute(theirs, "shot", swap)
    image = added(image, theirs)
    same_side = [
        [(2 * q + c) * groups + n for q in range(pairs) for n in range(groups)] for c in range(2)
    ]
    received = lax.all_to_all(
        image, ("shot", "beam"), split_axis=0, concat_axis=0, tiled=True,
        axis_index_groups=same_side,
    )

    tile_count = tile_owner.shape[0]
    tiles_each = tile_count // (shots * groups)
    numbers = jnp.arange(tile_count, dtype=i32)
    mine = tile_owner == shot_id * groups + group_id
    rank = jnp.sum((mine[None, :] & (numbers[None, :] < numbers[:, None])).astype(i32), axis=1)
    named = jnp.any(
        foot_tiles.reshape(groups, -1, 1) == numbers[None, None, :], axis=1
    )
    slot = jnp.sum(jnp.where(named & mine[None, :], rank[None, :], 0), axis=1)
    chosen = slot[None, :] == jnp.arange(tiles_each, dtype=i32)[:, None]
    received = received.reshape((pairs, groups) + received.shape[1:]).astype(jnp.float32)
    received = jnp.sum(received, axis=0)
    return jnp.sum(jnp.where(chosen[:, :, None, None], received[None], 0.0), axis=1)


def solution(mesh):
    in_specs = (
        P("shot", "beam", None),
        P("shot", None, None, None),
        P("shot", "beam", None),
        P("shot", "beam", None, None),
        P("beam", None, None),
        P("beam", None, None),
        P("beam", None),
        P("beam", None),
        P(),
        P(),
    )
    out_specs = P(("shot", "beam"), None, None)
    return jax.shard_map(body, mesh=mesh, in_specs=in_specs, out_specs=out_specs, check_vma=False)
```

```python
import functools
import math

import jax
import jax.numpy as jnp
import numpy as np
from jax import lax
from jax.experimental import pallas as pl
from jax.experimental.pallas import tpu as pltpu
from jax.sharding import PartitionSpec as P

FREQUENCIES = 64
DIRECTIONS = 32
WINDOW = 32
LANES = 128
FIRST_HZ = 4.0
STEP_HZ = 60.0 / FREQUENCIES
SPANS = LANES // DIRECTIONS
STEPS = FREQUENCIES // SPANS
PARTS = 2
BLOCK = PARTS * LANES
CHUNKS = 8
CHUNK_STEPS = STEPS // CHUNKS
TIE = CHUNKS - 2
ROWS = 16


LONGEST = 0.25


def fit_half_turn(reach, sine_terms, cosine_terms):
    nodes = reach * np.cos((np.arange(400) + 0.5) * np.pi / 800)
    u = nodes * nodes
    sine = np.polynomial.polynomial.polyfit(u, np.sin(np.pi * nodes) / nodes, sine_terms - 1)
    cosine = np.polynomial.polynomial.polyfit(u, np.cos(np.pi * nodes), cosine_terms - 1)
    return [float(v) for v in sine], [float(v) for v in cosine]


WIDE = fit_half_turn(0.5, 5, 5)
NARROW = fit_half_turn(STEP_HZ * LONGEST, 4, 4)


def horner(coefficients, u):
    total = coefficients[-1]
    for value in coefficients[-2::-1]:
        total = total * u + value
    return total


def half_turn(r, fits):
    u = r * r
    return horner(fits[1], u), r * horner(fits[0], u)


def first_phase(times):
    c, s = half_turn(FIRST_HZ * times - 0.5, WIDE)
    twice = s + s
    return twice * s - 1.0, -(twice * c)


def step_phase(times):
    c, s = half_turn(STEP_HZ * times, NARROW)
    twice = s + s
    return 1.0 - twice * s, twice * c


def span_phase(c, s):
    for _ in range(STEPS.bit_length() - 1):
        twice = s + s
        c, s = 1.0 - twice * s, twice * c
    return c, s


def stack_tables():
    freq = np.arange(FREQUENCIES, dtype=np.float32)
    angular = (2.0 * math.pi * (4.0 + 60.0 * freq / FREQUENCIES)).astype(np.float32)
    centred = (np.arange(WINDOW) - 0.5 * (WINDOW - 1)).astype(np.float32)
    taper = (np.exp(-((centred / (0.25 * WINDOW)) ** 2)) / math.sqrt(WINDOW)).astype(np.float32)
    slowness = (2e-05 * (np.arange(DIRECTIONS) - 0.5 * (DIRECTIONS - 1))).astype(np.float32)
    angle = angular[:, None, None] * slowness[None, :, None] * (25.0 * centred)[None, None, :]
    angle = angle.astype(np.float32)
    real = (taper * np.cos(angle)).astype(jnp.bfloat16).astype(np.float32)
    imag = (-taper * np.sin(angle)).astype(jnp.bfloat16).astype(np.float32)

    def lay(table):
        table = table.reshape(SPANS, STEPS, DIRECTIONS, WINDOW).transpose(1, 3, 0, 2)
        return np.ascontiguousarray(table.reshape(STEPS, WINDOW, LANES))

    return lay(real), lay(imag)


def pick_rows(table, held, across):
    outer, inner = table.shape
    count = outer * inner
    n = lax.broadcasted_iota(jnp.int32, (count, outer), 0)
    m = lax.broadcasted_iota(jnp.int32, (count, inner), 0)
    n, m = (lax.rem(n, outer), lax.div(m, outer)) if across else (lax.div(n, inner), lax.rem(m, inner))
    of_row = jnp.where(lax.broadcasted_iota(jnp.int32, (count, outer), 1) == n, 1.0, 0.0)
    halves = jnp.concatenate([lax.div(table, 256), lax.rem(table, 256)], axis=1)
    spread = jnp.dot(
        of_row.astype(jnp.bfloat16), halves.astype(jnp.float32).astype(jnp.bfloat16),
        preferred_element_type=jnp.float32,
    )
    spread = 256.0 * spread[:, :inner] + spread[:, inner:]
    kept = jnp.where(lax.broadcasted_iota(jnp.int32, (count, inner), 1) == m, spread, 0.0)
    number = jnp.sum(kept, axis=1, keepdims=True).astype(jnp.int32)
    choice = lax.broadcasted_iota(jnp.int32, (count, held.shape[0]), 1) == number
    choice = jnp.where(choice, 1.0, 0.0).astype(jnp.bfloat16)
    return jnp.dot(choice, held, preferred_element_type=jnp.float32).astype(jnp.bfloat16)


def route_kernel(table_ref, held_ref, out_ref):
    table = table_ref[0, lax.axis_index("beam")]
    out_ref[...] = pick_rows(table, held_ref[0], False).reshape(out_ref.shape)


def routed(table, held):
    return pl.pallas_call(
        route_kernel,
        out_shape=jax.ShapeDtypeStruct(table.shape[2:] + held.shape[2:], held.dtype),
        compiler_params=pltpu.CompilerParams(vmem_limit_bytes=61 << 20),
        name="routed",
    )(table, held)


def beam_kernel(slot_ref, arrived_ref, real_ref, imag_ref, out_ref):
    centres = out_ref.shape[0]
    windows = pick_rows(slot_ref[0], arrived_ref[...], True)
    scale = 1.0 / math.sqrt(DIRECTIONS * FREQUENCIES)
    row = lax.broadcasted_iota(jnp.int32, (PARTS * FREQUENCIES, BLOCK), 0)
    col = lax.broadcasted_iota(jnp.int32, (PARTS * FREQUENCIES, BLOCK), 1)
    home = lax.div(col, LANES) * FREQUENCIES + lax.div(lax.rem(col, LANES), DIRECTIONS) * STEPS
    for step in range(STEPS):
        pick = jnp.where(row == home + step, 1.0, 0.0).astype(jnp.bfloat16)
        spread = jnp.dot(windows, pick, preferred_element_type=jnp.float32)
        real = jnp.zeros((centres, LANES), jnp.float32)
        imag = jnp.zeros((centres, LANES), jnp.float32)
        for k in range(WINDOW):
            tr = spread[k * centres : (k + 1) * centres, :LANES]
            ti = spread[k * centres : (k + 1) * centres, LANES:]
            sr = real_ref[step, k : k + 1, :]
            si = imag_ref[step, k : k + 1, :]
            real = real + (sr * tr - si * ti)
            imag = imag + (sr * ti + si * tr)
        out_ref[:, 2 * step, :] = real * scale
        out_ref[:, 2 * step + 1, :] = imag * scale


def beams(slots, arrived, centres):
    real, imag = stack_tables()
    return pl.pallas_call(
        beam_kernel,
        out_shape=jax.ShapeDtypeStruct((centres, PARTS * STEPS, LANES), jnp.float32),
        compiler_params=pltpu.CompilerParams(vmem_limit_bytes=16 << 20),
        name="beams",
    )(slots, arrived, real, imag)


def start_phases(times, start_ref, shot):
    c, s = first_phase(times)
    step_c, step_s = step_phase(times)
    span_c, span_s = span_phase(step_c, step_s)
    cs, ss = [c], [s]
    for _ in range(SPANS - 1):
        c, s = c * span_c - s * span_s, c * span_s + s * span_c
        cs.append(c)
        ss.append(s)
    mark = None
    for n, pieces in enumerate((cs, ss, [step_c] * SPANS, [step_s] * SPANS)):
        turned = jnp.concatenate(pieces, axis=0).T
        start_ref[shot, n] = turned
        last = turned[-ROWS:]
        mark = last if mark is None else mark + last
    return mark


def start_lateral(lateral, spread, side_ref):
    def damped(hz, phase):
        damping = jnp.exp((-2.0 * math.pi * hz) * spread)
        return damping * phase[0], -(damping * phase[1])

    re, im = damped(FIRST_HZ, first_phase(lateral))
    step_re, step_im = damped(STEP_HZ, step_phase(lateral))
    side_ref[SPANS, 0], side_ref[SPANS, 1] = step_re, step_im
    span_re, span_im = step_re, step_im
    for _ in range(STEPS.bit_length() - 1):
        span_re, span_im = span_re * span_re - span_im * span_im, 2.0 * (span_re * span_im)
    for span in range(SPANS):
        side_ref[span, 0], side_ref[span, 1] = re, im
        re, im = re * span_re - im * span_im, re * span_im + im * span_re


def depth_chunk(chunk, centre, beam_refs, start_ref, state_ref, factor_ref, marks):
    cells = start_ref.shape[2]
    for block in range(cells // ROWS):
        rows = pl.ds(block * ROWS, ROWS)
        state = []
        for shot in range(2):
            if chunk == 0:
                c0 = start_ref[shot, 0, rows, :]
                s0 = start_ref[shot, 1, rows, :]
                sc = start_ref[shot, 2, rows, :]
                ss = start_ref[shot, 3, rows, :]
                c1, s1 = c0 * sc - s0 * ss, s0 * sc + c0 * ss
                twice = 2.0 * sc
                state_ref[shot, 4, rows, :] = twice
            else:
                c0, s0, c1, s1, twice = [state_ref[shot, n, rows, :] for n in range(5)]
                if chunk == TIE and block == 0:
                    c0 = jnp.where(marks[shot] > 100.0, marks[shot], c0)
            state.append((c0, s0, c1, s1, twice))
        for inner in range(CHUNK_STEPS):
            step = chunk * CHUNK_STEPS + inner
            re = im = None
            for shot in range(2):
                c0, s0, c1, s1, twice = state[shot]
                br = beam_refs[shot][centre, 2 * step : 2 * step + 1, :]
                bi = beam_refs[shot][centre, 2 * step + 1 : 2 * step + 2, :]
                part_re = br * c0 - bi * s0
                part_im = br * s0 + bi * c0
                re = part_re if re is None else re + part_re
                im = part_im if im is None else im + part_im
                state[shot] = (c1, s1, twice * c1 - c0, twice * s1 - s0, twice)
            col = inner * BLOCK
            factor_ref[rows, col : col + LANES] = re.astype(jnp.bfloat16)
            factor_ref[rows, col + LANES : col + BLOCK] = im.astype(jnp.bfloat16)
        if chunk + 1 < CHUNKS:
            for shot in range(2):
                for n in range(4):
                    state_ref[shot, n, rows, :] = state[shot][n]


def lateral_chunk(chunk, side_ref, chain_ref, factor_ref):
    source = side_ref if chunk == 0 else chain_ref
    step_re, step_im = side_ref[SPANS, 0], side_ref[SPANS, 1]
    if chunk == 0:
        chain_ref[SPANS, 0], chain_ref[SPANS, 1] = step_re, step_im
    else:
        step_re, step_im = chain_ref[SPANS, 0], chain_ref[SPANS, 1]
    for span in range(SPANS):
        re, im = source[span, 0], source[span, 1]
        for inner in range(CHUNK_STEPS):
            at = inner * BLOCK + span * DIRECTIONS
            factor_ref[at : at + DIRECTIONS, :] = re.astype(jnp.bfloat16)
            factor_ref[at + LANES : at + LANES + DIRECTIONS, :] = im.astype(jnp.bfloat16)
            if chunk * CHUNK_STEPS + inner + 1 < STEPS:
                re, im = re * step_re - im * step_im, re * step_im + im * step_re
        if chunk + 1 < CHUNKS:
            chain_ref[span, 0], chain_ref[span, 1] = re, im


def product(chunk, depth_factors, lateral_factors):
    return jnp.dot(
        depth_factors[chunk % 2][...],
        lateral_factors[chunk % 2][...],
        preferred_element_type=jnp.float32,
    )


def one_entry(
    centre, tile, last_tile, next_ref, beam_refs, image_ref, start_ref, state_ref, side_ref,
    chain_ref, depth_factors, lateral_factors,
):
    total, marks = None, []
    for chunk in range(CHUNKS):
        part = product(chunk - 1, depth_factors, lateral_factors)
        if chunk == 0:
            image_ref[last_tile] = image_ref[last_tile] + part
        else:
            total = part if total is None else total + part
        depth_chunk(
            chunk, centre, beam_refs, start_ref, state_ref, depth_factors[chunk % 2], marks
        )
        lateral_chunk(chunk, side_ref, chain_ref, lateral_factors[chunk % 2])
        if chunk < 2:
            marks.append(start_phases(next_ref[chunk], start_ref, chunk))
        if chunk == 2:
            start_lateral(next_ref[2], next_ref[3], side_ref)
    image_ref[tile] = image_ref[tile] + total


def steps_on(entry, counts):
    centre, slot = entry
    return settle(centre, slot + 2, counts, 2)


def settle(centre, slot, counts, most):
    for _ in range(most):
        held = counts[0, jnp.minimum(centre, counts.shape[1] - 1)]
        over = slot >= held
        slot = jnp.where(over, slot - held, slot)
        centre = jnp.where(over, centre + 1, centre)
    return centre, slot


def ray_row(entry, index_ref):
    centres, slots = index_ref.shape
    return index_ref[jnp.minimum(entry[0], centres - 1), jnp.minimum(entry[1], slots - 1)]


def first_entry(counts):
    side = lax.rem(lax.axis_index("shot"), 2)
    return settle(jnp.int32(0), side, counts, 1)


def first_kernel(
    count_ref, index_ref, own_ref, other_ref, lateral_ref, spread_ref, start_ref, side_ref,
    times_ref, sems,
):
    row = ray_row(first_entry(count_ref), index_ref)
    copies = first_times(row, (own_ref, other_ref, lateral_ref, spread_ref), times_ref, sems)
    for copy in copies:
        copy.start()
    for copy in copies:
        copy.wait()
    for shot in range(2):
        start_phases(times_ref[shot], start_ref, shot)
    start_lateral(times_ref[2], times_ref[3], side_ref)


def first_times(row, tables, times_ref, sems):
    return [
        pltpu.make_async_copy(table.at[row], times_ref.at[kind], sems.at[kind])
        for kind, table in enumerate(tables)
    ]


def first_of(foot_count, ray_index, tables):
    cells, across = tables[0].shape[2], tables[2].shape[2]
    scalars = pl.BlockSpec(memory_space=pltpu.SMEM)
    inside = pl.BlockSpec(memory_space=pltpu.VMEM)
    outside = pl.BlockSpec(memory_space=pltpu.HBM)
    anywhere = pl.BlockSpec(memory_space=pl.ANY)
    return pl.pallas_call(
        first_kernel,
        in_specs=[scalars] * 2 + [outside, anywhere, outside, outside],
        out_specs=[inside, inside],
        scratch_shapes=[
            pltpu.VMEM((4,) + tables[0].shape[1:], jnp.float32),
            pltpu.SemaphoreType.DMA((4,)),
        ],
        out_shape=[
            jax.ShapeDtypeStruct((2, 4, cells, LANES), jnp.float32),
            jax.ShapeDtypeStruct((SPANS + 1, 2, DIRECTIONS, across), jnp.float32),
        ],
        compiler_params=pltpu.CompilerParams(vmem_limit_bytes=61 << 20),
        name="first_of",
    )(foot_count, ray_index, *tables)


def tile_kernel(
    count_ref, index_ref, tiles_ref, owner_ref, first_start, first_side, own_beam, other_beam,
    own_ref, other_ref, lateral_ref, spread_ref, mine_ref, theirs_ref, image_ref, start_ref,
    state_ref, side_ref, chain_ref, depth_even, depth_odd, lateral_even, lateral_odd, times_ref,
    beams_ref, sems, first_sems,
):
    group, side = lax.axis_index("beam"), lax.rem(lax.axis_index("shot"), 2)
    groups = lax.axis_size("beam")
    half = mine_ref.shape[0]
    centres, slots = index_ref.shape
    found = count_ref[0, 0]
    for n in range(1, centres):
        found = found + count_ref[0, n]
    count = lax.div(found - side + 1, 2)
    depth_factors, lateral_factors = (depth_even, depth_odd), (lateral_even, lateral_odd)
    tables = (own_ref, other_ref, lateral_ref, spread_ref)

    def times(entry, slot):
        return first_times(ray_row(entry, index_ref), tables, times_ref.at[slot], sems.at[slot])

    def fetch(entry, slot):
        for copy in times(entry, slot):
            copy.start()

    def arrive(entry, slot):
        for copy in times(entry, slot):
            copy.wait()

    def tile_of(entry):
        owner = owner_ref[tiles_ref[(group * centres + entry[0]) * slots + entry[1]]]
        shot, home = lax.div(owner, groups), lax.rem(owner, groups)
        away = jnp.where(lax.rem(shot, 2) == side, 0, half)
        return lax.div(shot, 2) * groups + home + away

    def one(n, carry):
        entry, later, last = carry
        slot = lax.rem(n, 2)
        after = steps_on(later, count_ref)
        arrive(later, 1 - slot)
        fetch(after, slot)
        tile = tile_of(entry)
        one_entry(
            entry[0], tile, last, times_ref.at[1 - slot], (beams_ref.at[0], beams_ref.at[1]), image_ref,
            start_ref, state_ref, side_ref, chain_ref, depth_factors, lateral_factors,
        )
        return later, after, tile

    first = first_entry(count_ref)
    second = steps_on(first, count_ref)
    fetch(second, 1)
    arriving = [
        pltpu.make_async_copy(source, target, first_sems.at[n])
        for n, (source, target) in enumerate(
            (
                (own_beam, beams_ref.at[0]), (other_beam, beams_ref.at[1]),
                (first_start, start_ref), (first_side, side_ref),
            )
        )
    ]
    for copy in arriving:
        copy.start()
    image_ref[...] = jnp.zeros_like(image_ref)
    depth_odd[...] = jnp.zeros_like(depth_odd)
    lateral_odd[...] = jnp.zeros_like(lateral_odd)
    for copy in arriving:
        copy.wait()
    _, later, last = lax.fori_loop(0, count, one, (first, second, jnp.int32(0)))
    arrive(later, lax.rem(count + 1, 2))
    part = product(CHUNKS - 1, depth_factors, lateral_factors)
    image_ref[last] = image_ref[last] + part
    mine_ref[...] = image_ref[:half].astype(mine_ref.dtype)
    theirs_ref[...] = image_ref[half:].astype(theirs_ref.dtype)


def tiles_of(entries, firsts, beams, tables, tiles):
    cells, across = tables[0].shape[2], tables[2].shape[2]
    scalars = pl.BlockSpec(memory_space=pltpu.SMEM)
    inside = pl.BlockSpec(memory_space=pltpu.VMEM)
    outside = pl.BlockSpec(memory_space=pltpu.HBM)
    anywhere = pl.BlockSpec(memory_space=pl.ANY)
    return pl.pallas_call(
        tile_kernel,
        in_specs=[scalars] * 4 + [anywhere] * 4 + [outside, anywhere, outside, outside],
        out_specs=[inside] * 2,
        scratch_shapes=[
            pltpu.VMEM((2 * tiles, cells, across), jnp.float32),
            pltpu.VMEM((2, 4, cells, LANES), jnp.float32),
            pltpu.VMEM((2, 5, cells, LANES), jnp.float32),
            pltpu.VMEM((SPANS + 1, 2, DIRECTIONS, across), jnp.float32),
            pltpu.VMEM((SPANS + 1, 2, DIRECTIONS, across), jnp.float32),
            pltpu.VMEM((cells, CHUNK_STEPS * BLOCK), jnp.bfloat16),
            pltpu.VMEM((cells, CHUNK_STEPS * BLOCK), jnp.bfloat16),
            pltpu.VMEM((CHUNK_STEPS * BLOCK, across), jnp.bfloat16),
            pltpu.VMEM((CHUNK_STEPS * BLOCK, across), jnp.bfloat16),
            pltpu.VMEM((2, 4) + tables[0].shape[1:], jnp.float32),
            pltpu.VMEM((2,) + beams[0].shape, jnp.float32),
            pltpu.SemaphoreType.DMA((2, 4)),
            pltpu.SemaphoreType.DMA((4,)),
        ],
        out_shape=[
            jax.ShapeDtypeStruct((tiles, cells, across), kind)
            for kind in (jnp.bfloat16, jnp.bfloat16)
        ],
        compiler_params=pltpu.CompilerParams(vmem_limit_bytes=50 << 20),
        cost_estimate=pl.CostEstimate(
            flops=40_000_000_000, transcendentals=0, bytes_accessed=4_000_000
        ),
        name="tiles_of",
    )(*entries, *firsts, *beams, *tables)


def add_kernel(one_ref, other_ref, out_ref):
    total = one_ref[...].astype(jnp.float32) + other_ref[...].astype(jnp.float32)
    out_ref[...] = total.astype(out_ref.dtype)


def added(one, other):
    return pl.pallas_call(
        add_kernel,
        out_shape=jax.ShapeDtypeStruct(one.shape, one.dtype),
        compiler_params=pltpu.CompilerParams(vmem_limit_bytes=16 << 20),
        name="added",
    )(one, other)


def body(
    traces, send_table, window_slots, ray_depth, ray_lateral, ray_spread,
    ray_index, foot_count, foot_tiles, tile_owner,
):
    groups = lax.axis_size("beam")
    shots = lax.axis_size("shot")
    pairs = shots // 2
    group_id = lax.axis_index("beam")
    shot_id = lax.axis_index("shot")
    swap = [(n, n ^ 1) for n in range(shots)]
    i32 = jnp.int32

    own_depth = ray_depth[0]
    other_depth = lax.ppermute(own_depth, "shot", swap)

    sent = routed(send_table, traces)
    arrived = lax.all_to_all(sent, "beam", split_axis=0, concat_axis=0, tiled=True)
    arrived = arrived.reshape(-1, arrived.shape[-1])
    tables = (own_depth, other_depth, ray_lateral, ray_spread)
    firsts = first_of(foot_count, ray_index, tables)
    arrived, firsts, flat_tiles = lax.optimization_barrier(
        (arrived, firsts, foot_tiles.reshape(-1))
    )
    entries = (foot_count, ray_index, flat_tiles, tile_owner)
    own_beam = beams(window_slots, arrived, window_slots.shape[1])
    other_beam = lax.ppermute(own_beam, "shot", swap)

    image, theirs = tiles_of(entries, firsts, (own_beam, other_beam), tables, pairs * groups)
    theirs = lax.ppermute(theirs, "shot", swap)
    image = added(image, theirs)
    same_side = [
        [(2 * q + c) * groups + n for q in range(pairs) for n in range(groups)] for c in range(2)
    ]
    received = lax.all_to_all(
        image, ("shot", "beam"), split_axis=0, concat_axis=0, tiled=True,
        axis_index_groups=same_side,
    )

    tile_count = tile_owner.shape[0]
    tiles_each = tile_count // (shots * groups)
    numbers = jnp.arange(tile_count, dtype=i32)
    mine = tile_owner == shot_id * groups + group_id
    rank = jnp.sum((mine[None, :] & (numbers[None, :] < numbers[:, None])).astype(i32), axis=1)
    named = jnp.any(
        foot_tiles.reshape(groups, -1, 1) == numbers[None, None, :], axis=1
    )
    slot = jnp.sum(jnp.where(named & mine[None, :], rank[None, :], 0), axis=1)
    chosen = slot[None, :] == jnp.arange(tiles_each, dtype=i32)[:, None]
    received = received.reshape((pairs, groups) + received.shape[1:]).astype(jnp.float32)
    received = jnp.sum(received, axis=0)
    return jnp.sum(jnp.where(chosen[:, :, None, None], received[None], 0.0), axis=1)


def solution(mesh):
    in_specs = (
        P("shot", "beam", None),
        P("shot", None, None, None),
        P("shot", "beam", None),
        P("shot", "beam", None, None),
        P("beam", None, None),
        P("beam", None, None),
        P("beam", None),
        P("beam", None),
        P(),
        P(),
    )
    out_specs = P(("shot", "beam"), None, None)
    return jax.shard_map(body, mesh=mesh, in_specs=in_specs, out_specs=out_specs, check_vma=False)
```

```python
import functools
import math

import jax
import jax.numpy as jnp
import numpy as np
from jax import lax
from jax.experimental import pallas as pl
from jax.experimental.pallas import tpu as pltpu
from jax.sharding import PartitionSpec as P

FREQUENCIES = 64
DIRECTIONS = 32
WINDOW = 32
LANES = 128
FIRST_HZ = 4.0
STEP_HZ = 60.0 / FREQUENCIES
SPANS = LANES // DIRECTIONS
STEPS = FREQUENCIES // SPANS
PARTS = 2
BLOCK = PARTS * LANES
CHUNKS = 8
CHUNK_STEPS = STEPS // CHUNKS
TIE = CHUNKS - 2
ROWS = 16


LONGEST = 0.25


def fit_half_turn(reach, sine_terms, cosine_terms):
    nodes = reach * np.cos((np.arange(400) + 0.5) * np.pi / 800)
    u = nodes * nodes
    sine = np.polynomial.polynomial.polyfit(u, np.sin(np.pi * nodes) / nodes, sine_terms - 1)
    cosine = np.polynomial.polynomial.polyfit(u, np.cos(np.pi * nodes), cosine_terms - 1)
    return [float(v) for v in sine], [float(v) for v in cosine]


WIDE = fit_half_turn(0.5, 5, 5)
NARROW = fit_half_turn(STEP_HZ * LONGEST, 4, 4)


def horner(coefficients, u):
    total = coefficients[-1]
    for value in coefficients[-2::-1]:
        total = total * u + value
    return total


def half_turn(r, fits):
    u = r * r
    return horner(fits[1], u), r * horner(fits[0], u)


def first_phase(times):
    c, s = half_turn(FIRST_HZ * times - 0.5, WIDE)
    twice = s + s
    return twice * s - 1.0, -(twice * c)


def step_phase(times):
    c, s = half_turn(STEP_HZ * times, NARROW)
    twice = s + s
    return 1.0 - twice * s, twice * c


def span_phase(c, s):
    for _ in range(STEPS.bit_length() - 1):
        twice = s + s
        c, s = 1.0 - twice * s, twice * c
    return c, s


def stack_tables():
    freq = np.arange(FREQUENCIES, dtype=np.float32)
    angular = (2.0 * math.pi * (4.0 + 60.0 * freq / FREQUENCIES)).astype(np.float32)
    centred = (np.arange(WINDOW) - 0.5 * (WINDOW - 1)).astype(np.float32)
    taper = (np.exp(-((centred / (0.25 * WINDOW)) ** 2)) / math.sqrt(WINDOW)).astype(np.float32)
    slowness = (2e-05 * (np.arange(DIRECTIONS) - 0.5 * (DIRECTIONS - 1))).astype(np.float32)
    angle = angular[:, None, None] * slowness[None, :, None] * (25.0 * centred)[None, None, :]
    angle = angle.astype(np.float32)
    real = (taper * np.cos(angle)).astype(jnp.bfloat16).astype(np.float32)
    imag = (-taper * np.sin(angle)).astype(jnp.bfloat16).astype(np.float32)

    def lay(table):
        table = table.reshape(SPANS, STEPS, DIRECTIONS, WINDOW).transpose(1, 3, 0, 2)
        return np.ascontiguousarray(table.reshape(STEPS, WINDOW, LANES))

    return lay(real), lay(imag)


def pick_rows(table, held, across):
    outer, inner = table.shape
    count = outer * inner
    n = lax.broadcasted_iota(jnp.int32, (count, outer), 0)
    m = lax.broadcasted_iota(jnp.int32, (count, inner), 0)
    n, m = (lax.rem(n, outer), lax.div(m, outer)) if across else (lax.div(n, inner), lax.rem(m, inner))
    of_row = jnp.where(lax.broadcasted_iota(jnp.int32, (count, outer), 1) == n, 1.0, 0.0)
    halves = jnp.concatenate([lax.div(table, 256), lax.rem(table, 256)], axis=1)
    spread = jnp.dot(
        of_row.astype(jnp.bfloat16), halves.astype(jnp.float32).astype(jnp.bfloat16),
        preferred_element_type=jnp.float32,
    )
    spread = 256.0 * spread[:, :inner] + spread[:, inner:]
    kept = jnp.where(lax.broadcasted_iota(jnp.int32, (count, inner), 1) == m, spread, 0.0)
    number = jnp.sum(kept, axis=1, keepdims=True).astype(jnp.int32)
    choice = lax.broadcasted_iota(jnp.int32, (count, held.shape[0]), 1) == number
    choice = jnp.where(choice, 1.0, 0.0).astype(jnp.bfloat16)
    return jnp.dot(choice, held, preferred_element_type=jnp.float32).astype(jnp.bfloat16)


def route_kernel(table_ref, held_ref, out_ref):
    table = table_ref[0, lax.axis_index("beam")]
    out_ref[...] = pick_rows(table, held_ref[0], False).reshape(out_ref.shape)


def routed(table, held):
    return pl.pallas_call(
        route_kernel,
        out_shape=jax.ShapeDtypeStruct(table.shape[2:] + held.shape[2:], held.dtype),
        compiler_params=pltpu.CompilerParams(vmem_limit_bytes=61 << 20),
        name="routed",
    )(table, held)


def beam_kernel(slot_ref, arrived_ref, real_ref, imag_ref, out_ref):
    centres = out_ref.shape[0]
    windows = pick_rows(slot_ref[0], arrived_ref[...], True)
    scale = 1.0 / math.sqrt(DIRECTIONS * FREQUENCIES)
    row = lax.broadcasted_iota(jnp.int32, (PARTS * FREQUENCIES, BLOCK), 0)
    col = lax.broadcasted_iota(jnp.int32, (PARTS * FREQUENCIES, BLOCK), 1)
    home = lax.div(col, LANES) * FREQUENCIES + lax.div(lax.rem(col, LANES), DIRECTIONS) * STEPS
    for step in range(STEPS):
        pick = jnp.where(row == home + step, 1.0, 0.0).astype(jnp.bfloat16)
        spread = jnp.dot(windows, pick, preferred_element_type=jnp.float32)
        real = jnp.zeros((centres, LANES), jnp.float32)
        imag = jnp.zeros((centres, LANES), jnp.float32)
        for k in range(WINDOW):
            tr = spread[k * centres : (k + 1) * centres, :LANES]
            ti = spread[k * centres : (k + 1) * centres, LANES:]
            sr = real_ref[step, k : k + 1, :]
            si = imag_ref[step, k : k + 1, :]
            real = real + (sr * tr - si * ti)
            imag = imag + (sr * ti + si * tr)
        out_ref[:, 2 * step, :] = real * scale
        out_ref[:, 2 * step + 1, :] = imag * scale


def beams(slots, arrived, centres):
    real, imag = stack_tables()
    return pl.pallas_call(
        beam_kernel,
        out_shape=jax.ShapeDtypeStruct((centres, PARTS * STEPS, LANES), jnp.float32),
        compiler_params=pltpu.CompilerParams(vmem_limit_bytes=16 << 20),
        name="beams",
    )(slots, arrived, real, imag)


def start_phases(times, start_ref, shot):
    c, s = first_phase(times)
    step_c, step_s = step_phase(times)
    span_c, span_s = span_phase(step_c, step_s)
    cs, ss = [c], [s]
    for _ in range(SPANS - 1):
        c, s = c * span_c - s * span_s, c * span_s + s * span_c
        cs.append(c)
        ss.append(s)
    mark = None
    for n, pieces in enumerate((cs, ss, [step_c] * SPANS, [step_s] * SPANS)):
        turned = jnp.concatenate(pieces, axis=0).T
        start_ref[shot, n] = turned
        last = turned[-ROWS:]
        mark = last if mark is None else mark + last
    return mark


def start_lateral(lateral, spread, side_ref):
    def damped(hz, phase):
        damping = jnp.exp((-2.0 * math.pi * hz) * spread)
        return damping * phase[0], -(damping * phase[1])

    re, im = damped(FIRST_HZ, first_phase(lateral))
    step_re, step_im = damped(STEP_HZ, step_phase(lateral))
    side_ref[SPANS, 0], side_ref[SPANS, 1] = step_re, step_im
    span_re, span_im = step_re, step_im
    for _ in range(STEPS.bit_length() - 1):
        span_re, span_im = span_re * span_re - span_im * span_im, 2.0 * (span_re * span_im)
    for span in range(SPANS):
        side_ref[span, 0], side_ref[span, 1] = re, im
        re, im = re * span_re - im * span_im, re * span_im + im * span_re


def depth_chunk(chunk, centre, beam_refs, start_ref, state_ref, factor_ref, marks):
    cells = start_ref.shape[2]
    for block in range(cells // ROWS):
        rows = pl.ds(block * ROWS, ROWS)
        state = []
        for shot in range(2):
            if chunk == 0:
                c0 = start_ref[shot, 0, rows, :]
                s0 = start_ref[shot, 1, rows, :]
                sc = start_ref[shot, 2, rows, :]
                ss = start_ref[shot, 3, rows, :]
                c1, s1 = c0 * sc - s0 * ss, s0 * sc + c0 * ss
                twice = 2.0 * sc
                state_ref[shot, 4, rows, :] = twice
            else:
                c0, s0, c1, s1, twice = [state_ref[shot, n, rows, :] for n in range(5)]
                if chunk == TIE and block == 0:
                    c0 = jnp.where(marks[shot] > 100.0, marks[shot], c0)
            state.append((c0, s0, c1, s1, twice))
        for inner in range(CHUNK_STEPS):
            step = chunk * CHUNK_STEPS + inner
            re = im = None
            for shot in range(2):
                c0, s0, c1, s1, twice = state[shot]
                br = beam_refs[shot][centre, 2 * step : 2 * step + 1, :]
                bi = beam_refs[shot][centre, 2 * step + 1 : 2 * step + 2, :]
                part_re = br * c0 - bi * s0
                part_im = br * s0 + bi * c0
                re = part_re if re is None else re + part_re
                im = part_im if im is None else im + part_im
                state[shot] = (c1, s1, twice * c1 - c0, twice * s1 - s0, twice)
            col = inner * BLOCK
            factor_ref[rows, col : col + LANES] = re.astype(jnp.bfloat16)
            factor_ref[rows, col + LANES : col + BLOCK] = im.astype(jnp.bfloat16)
        if chunk + 1 < CHUNKS:
            for shot in range(2):
                for n in range(4):
                    state_ref[shot, n, rows, :] = state[shot][n]


def lateral_chunk(chunk, side_ref, chain_ref, factor_ref):
    source = side_ref if chunk == 0 else chain_ref
    step_re, step_im = side_ref[SPANS, 0], side_ref[SPANS, 1]
    if chunk == 0:
        chain_ref[SPANS, 0], chain_ref[SPANS, 1] = step_re, step_im
    else:
        step_re, step_im = chain_ref[SPANS, 0], chain_ref[SPANS, 1]
    for span in range(SPANS):
        re, im = source[span, 0], source[span, 1]
        for inner in range(CHUNK_STEPS):
            at = inner * BLOCK + span * DIRECTIONS
            factor_ref[at : at + DIRECTIONS, :] = re.astype(jnp.bfloat16)
            factor_ref[at + LANES : at + LANES + DIRECTIONS, :] = im.astype(jnp.bfloat16)
            if chunk * CHUNK_STEPS + inner + 1 < STEPS:
                re, im = re * step_re - im * step_im, re * step_im + im * step_re
        if chunk + 1 < CHUNKS:
            chain_ref[span, 0], chain_ref[span, 1] = re, im


def product(chunk, depth_factors, lateral_factors):
    return jnp.dot(
        depth_factors[chunk % 2][...],
        lateral_factors[chunk % 2][...],
        preferred_element_type=jnp.float32,
    )


def one_entry(
    centre, tile, last_tile, next_ref, beam_refs, image_ref, start_ref, state_ref, side_ref,
    chain_ref, depth_factors, lateral_factors,
):
    total, marks = None, []
    for chunk in range(CHUNKS):
        part = product(chunk - 1, depth_factors, lateral_factors)
        if chunk == 0:
            image_ref[last_tile] = image_ref[last_tile] + part
        else:
            total = part if total is None else total + part
        depth_chunk(
            chunk, centre, beam_refs, start_ref, state_ref, depth_factors[chunk % 2], marks
        )
        lateral_chunk(chunk, side_ref, chain_ref, lateral_factors[chunk % 2])
        if chunk < 2:
            marks.append(start_phases(next_ref[chunk], start_ref, chunk))
        if chunk == 2:
            start_lateral(next_ref[2], next_ref[3], side_ref)
    image_ref[tile] = image_ref[tile] + total


def steps_on(entry, counts):
    centre, slot = entry
    return settle(centre, slot + 2, counts, 2)


def settle(centre, slot, counts, most):
    for _ in range(most):
        held = counts[0, jnp.minimum(centre, counts.shape[1] - 1)]
        over = slot >= held
        slot = jnp.where(over, slot - held, slot)
        centre = jnp.where(over, centre + 1, centre)
    return centre, slot


def ray_row(entry, index_ref):
    centres, slots = index_ref.shape
    return index_ref[jnp.minimum(entry[0], centres - 1), jnp.minimum(entry[1], slots - 1)]


def first_entry(counts):
    side = lax.rem(lax.axis_index("shot"), 2)
    return settle(jnp.int32(0), side, counts, 1)


def first_kernel(
    count_ref, index_ref, own_ref, other_ref, lateral_ref, spread_ref, start_ref, side_ref,
    times_ref, sems,
):
    row = ray_row(first_entry(count_ref), index_ref)
    copies = first_times(row, (own_ref, other_ref, lateral_ref, spread_ref), times_ref, sems)
    for copy in copies:
        copy.start()
    for copy in copies:
        copy.wait()
    for shot in range(2):
        start_phases(times_ref[shot], start_ref, shot)
    start_lateral(times_ref[2], times_ref[3], side_ref)


def first_times(row, tables, times_ref, sems):
    return [
        pltpu.make_async_copy(table.at[row], times_ref.at[kind], sems.at[kind])
        for kind, table in enumerate(tables)
    ]


def first_of(foot_count, ray_index, tables):
    cells, across = tables[0].shape[2], tables[2].shape[2]
    scalars = pl.BlockSpec(memory_space=pltpu.SMEM)
    inside = pl.BlockSpec(memory_space=pltpu.VMEM)
    outside = pl.BlockSpec(memory_space=pltpu.HBM)
    anywhere = pl.BlockSpec(memory_space=pl.ANY)
    return pl.pallas_call(
        first_kernel,
        in_specs=[scalars] * 2 + [outside, anywhere, outside, outside],
        out_specs=[inside, inside],
        scratch_shapes=[
            pltpu.VMEM((4,) + tables[0].shape[1:], jnp.float32),
            pltpu.SemaphoreType.DMA((4,)),
        ],
        out_shape=[
            jax.ShapeDtypeStruct((2, 4, cells, LANES), jnp.float32),
            jax.ShapeDtypeStruct((SPANS + 1, 2, DIRECTIONS, across), jnp.float32),
        ],
        compiler_params=pltpu.CompilerParams(vmem_limit_bytes=61 << 20),
        name="first_of",
    )(foot_count, ray_index, *tables)


def tile_kernel(
    count_ref, index_ref, tiles_ref, owner_ref, first_start, first_side, own_beam, other_beam,
    own_ref, other_ref, lateral_ref, spread_ref, mine_ref, theirs_ref, image_ref, start_ref,
    state_ref, side_ref, chain_ref, depth_even, depth_odd, lateral_even, lateral_odd, times_ref,
    beams_ref, sems, first_sems,
):
    group, side = lax.axis_index("beam"), lax.rem(lax.axis_index("shot"), 2)
    groups = lax.axis_size("beam")
    half = mine_ref.shape[0]
    centres, slots = index_ref.shape
    found = count_ref[0, 0]
    for n in range(1, centres):
        found = found + count_ref[0, n]
    count = lax.div(found - side + 1, 2)
    depth_factors, lateral_factors = (depth_even, depth_odd), (lateral_even, lateral_odd)
    tables = (own_ref, other_ref, lateral_ref, spread_ref)

    def times(entry, slot):
        return first_times(ray_row(entry, index_ref), tables, times_ref.at[slot], sems.at[slot])

    def fetch(entry, slot):
        for copy in times(entry, slot):
            copy.start()

    def arrive(entry, slot):
        for copy in times(entry, slot):
            copy.wait()

    def tile_of(entry):
        owner = owner_ref[tiles_ref[(group * centres + entry[0]) * slots + entry[1]]]
        shot, home = lax.div(owner, groups), lax.rem(owner, groups)
        away = jnp.where(lax.rem(shot, 2) == side, 0, half)
        return lax.div(shot, 2) * groups + home + away

    def one(n, carry):
        entry, later, last = carry
        slot = lax.rem(n, 2)
        after = steps_on(later, count_ref)
        arrive(later, 1 - slot)
        fetch(after, slot)
        tile = tile_of(entry)
        one_entry(
            entry[0], tile, last, times_ref.at[1 - slot], (beams_ref.at[0], beams_ref.at[1]), image_ref,
            start_ref, state_ref, side_ref, chain_ref, depth_factors, lateral_factors,
        )
        return later, after, tile

    first = first_entry(count_ref)
    second = steps_on(first, count_ref)
    fetch(second, 1)
    arriving = [
        pltpu.make_async_copy(source, target, first_sems.at[n])
        for n, (source, target) in enumerate(
            (
                (own_beam, beams_ref.at[0]), (other_beam, beams_ref.at[1]),
                (first_start, start_ref), (first_side, side_ref),
            )
        )
    ]
    for copy in arriving:
        copy.start()
    image_ref[...] = jnp.zeros_like(image_ref)
    depth_odd[...] = jnp.zeros_like(depth_odd)
    lateral_odd[...] = jnp.zeros_like(lateral_odd)
    for copy in arriving:
        copy.wait()
    _, later, last = lax.fori_loop(0, count, one, (first, second, jnp.int32(0)))
    arrive(later, lax.rem(count + 1, 2))
    part = product(CHUNKS - 1, depth_factors, lateral_factors)
    image_ref[last] = image_ref[last] + part
    mine_ref[...] = image_ref[:half].astype(mine_ref.dtype)
    theirs_ref[...] = image_ref[half:].astype(theirs_ref.dtype)


def tiles_of(entries, firsts, beams, tables, tiles):
    cells, across = tables[0].shape[2], tables[2].shape[2]
    scalars = pl.BlockSpec(memory_space=pltpu.SMEM)
    inside = pl.BlockSpec(memory_space=pltpu.VMEM)
    outside = pl.BlockSpec(memory_space=pltpu.HBM)
    anywhere = pl.BlockSpec(memory_space=pl.ANY)
    return pl.pallas_call(
        tile_kernel,
        in_specs=[scalars] * 4 + [outside] * 3 + [anywhere, outside, anywhere, outside, outside],
        out_specs=[inside] * 2,
        scratch_shapes=[
            pltpu.VMEM((2 * tiles, cells, across), jnp.float32),
            pltpu.VMEM((2, 4, cells, LANES), jnp.float32),
            pltpu.VMEM((2, 5, cells, LANES), jnp.float32),
            pltpu.VMEM((SPANS + 1, 2, DIRECTIONS, across), jnp.float32),
            pltpu.VMEM((SPANS + 1, 2, DIRECTIONS, across), jnp.float32),
            pltpu.VMEM((cells, CHUNK_STEPS * BLOCK), jnp.bfloat16),
            pltpu.VMEM((cells, CHUNK_STEPS * BLOCK), jnp.bfloat16),
            pltpu.VMEM((CHUNK_STEPS * BLOCK, across), jnp.bfloat16),
            pltpu.VMEM((CHUNK_STEPS * BLOCK, across), jnp.bfloat16),
            pltpu.VMEM((2, 4) + tables[0].shape[1:], jnp.float32),
            pltpu.VMEM((2,) + beams[0].shape, jnp.float32),
            pltpu.SemaphoreType.DMA((2, 4)),
            pltpu.SemaphoreType.DMA((4,)),
        ],
        out_shape=[
            jax.ShapeDtypeStruct((tiles, cells, across), kind)
            for kind in (jnp.bfloat16, jnp.bfloat16)
        ],
        compiler_params=pltpu.CompilerParams(vmem_limit_bytes=50 << 20),
        cost_estimate=pl.CostEstimate(
            flops=40_000_000_000, transcendentals=0, bytes_accessed=4_000_000
        ),
        name="tiles_of",
    )(*entries, *firsts, *beams, *tables)


def add_kernel(one_ref, other_ref, out_ref):
    total = one_ref[...].astype(jnp.float32) + other_ref[...].astype(jnp.float32)
    out_ref[...] = total.astype(out_ref.dtype)


def added(one, other):
    return pl.pallas_call(
        add_kernel,
        out_shape=jax.ShapeDtypeStruct(one.shape, one.dtype),
        compiler_params=pltpu.CompilerParams(vmem_limit_bytes=16 << 20),
        name="added",
    )(one, other)


def body(
    traces, send_table, window_slots, ray_depth, ray_lateral, ray_spread,
    ray_index, foot_count, foot_tiles, tile_owner,
):
    groups = lax.axis_size("beam")
    shots = lax.axis_size("shot")
    pairs = shots // 2
    group_id = lax.axis_index("beam")
    shot_id = lax.axis_index("shot")
    swap = [(n, n ^ 1) for n in range(shots)]
    i32 = jnp.int32

    own_depth = ray_depth[0]
    other_depth = lax.ppermute(own_depth, "shot", swap)

    sent = routed(send_table, traces)
    arrived = lax.all_to_all(sent, "beam", split_axis=0, concat_axis=0, tiled=True)
    arrived = arrived.reshape(-1, arrived.shape[-1])
    tables = (own_depth, other_depth, ray_lateral, ray_spread)
    firsts = first_of(foot_count, ray_index, tables)
    arrived, firsts, flat_tiles = lax.optimization_barrier(
        (arrived, firsts, foot_tiles.reshape(-1))
    )
    entries = (foot_count, ray_index, flat_tiles, tile_owner)
    own_beam = beams(window_slots, arrived, window_slots.shape[1])
    other_beam = lax.ppermute(own_beam, "shot", swap)

    image, theirs = tiles_of(entries, firsts, (own_beam, other_beam), tables, pairs * groups)
    theirs = lax.ppermute(theirs, "shot", swap)
    image = added(image, theirs)
    same_side = [
        [(2 * q + c) * groups + n for q in range(pairs) for n in range(groups)] for c in range(2)
    ]
    received = lax.all_to_all(
        image, ("shot", "beam"), split_axis=0, concat_axis=0, tiled=True,
        axis_index_groups=same_side,
    )

    tile_count = tile_owner.shape[0]
    tiles_each = tile_count // (shots * groups)
    numbers = jnp.arange(tile_count, dtype=i32)
    mine = tile_owner == shot_id * groups + group_id
    rank = jnp.sum((mine[None, :] & (numbers[None, :] < numbers[:, None])).astype(i32), axis=1)
    named = jnp.any(
        foot_tiles.reshape(groups, -1, 1) == numbers[None, None, :], axis=1
    )
    slot = jnp.sum(jnp.where(named & mine[None, :], rank[None, :], 0), axis=1)
    chosen = slot[None, :] == jnp.arange(tiles_each, dtype=i32)[:, None]
    received = received.reshape((pairs, groups) + received.shape[1:]).astype(jnp.float32)
    received = jnp.sum(received, axis=0)
    return jnp.sum(jnp.where(chosen[:, :, None, None], received[None], 0.0), axis=1)


def solution(mesh):
    in_specs = (
        P("shot", "beam", None),
        P("shot", None, None, None),
        P("shot", "beam", None),
        P("shot", "beam", None, None),
        P("beam", None, None),
        P("beam", None, None),
        P("beam", None),
        P("beam", None),
        P(),
        P(),
    )
    out_specs = P(("shot", "beam"), None, None)
    return jax.shard_map(body, mesh=mesh, in_specs=in_specs, out_specs=out_specs, check_vma=False)
```
